512 devices in a mesh: dp: 32 (over z, x), tensor: 16 (over y, core).
Axes of the slice: x: 4, y: 8, z: 8, core: 2. Of those that a mesh axis runs over, the one named last changes fastest.
Arguments:
- grads_out: bfloat16 [1024, 28672], P('dp'), may hold values from -6 to 6
- inputs: bfloat16 [1024, 8192], P('dp'), may hold values from -6 to 6
- basis_out: bfloat16 [28672, 14336], P('dp', 'tensor'), may hold values from -0.03125 to 0.03125
- basis_in: bfloat16 [8192, 4096], P('tensor', 'dp'), may hold values from -0.0625 to 0.0625
- lengths: int32 [32], P('dp'), may hold values from 1 to 32, as said below
Outputs:
- corrections: float32 [14336, 4096], P('tensor', 'dp')
The draws below stay inside these ranges and needn't reach their ends.
Inputs may be any that keep to these rules, and one draw needn't show every extreme that they name: `lengths`: every sequence has at least one live token, and some sequence has all 32 slots live.
All inputs are finite; a program needn't handle non-finite values.
Results may differ from the reference program's by a relative error of at most 0.0026.
Values may be sent and summed in bfloat16 or wider, within the bound.
No kernel may reach another device: no remote copies, remote signals or barrier semaphores. Data moves between devices by JAX's collectives and lax.ppermute only.
A program may use at most 64 MiB of HBM per device.

```python
import jax
import jax.numpy as jnp
from jax import lax

D = 8192
FF = 28672
FW = 14336
DW = 4096
LEN = 32
SEQS = 32
TOKENS = 1024


def draw_lengths(key, part):
    inner = jax.random.fold_in(key, 11)
    first_key, second_key = jax.random.split(inner)
    base = jax.random.randint(first_key, (SEQS,), 1, LEN + 1)
    chosen = jax.random.randint(second_key, (), 0, SEQS)
    return jnp.where(jnp.arange(SEQS) == chosen, LEN, base).astype(jnp.int32)


def level_of(key, dims, cuts, smallest, high):
    loudness = 1.0
    for dim, shards_of in cuts:
        steps = jax.random.uniform(jax.random.fold_in(jax.random.fold_in(key, 6), dim), (shards_of,), jnp.float32, smallest / len(cuts), high / len(cuts))
        loudness = loudness * jnp.repeat(jnp.exp(steps), dims[dim] // shards_of).reshape((-1,) + (1,) * (len(dims) - 1 - dim))
    return loudness


def normal_values(rng, extent, width, most, shards=(), kind=jnp.bfloat16):
    result = width * jax.random.normal(rng, extent, jnp.float32)
    if shards:
        result = result * level_of(rng, extent, shards, -0.22, 0.18)
    return jnp.clip(result, -most, most).astype(kind)


def setup_inputs(seed: int = 0) -> dict:
    seeds = jax.random.split(jax.random.key(seed), 6)
    grads_out = normal_values(seeds[0], (TOKENS, FF), 1.0, 6.0, ((0, 32),))
    inputs = normal_values(seeds[1], (TOKENS, D), 1.0, 6.0, ((0, 32),))
    basis_out = normal_values(seeds[2], (FF, FW), FF ** -0.5, 0.03125, ((0, 32), (1, 16)))
    basis_in = normal_values(seeds[3], (D, DW), D ** -0.5, 0.0625, ((0, 16), (1, 32)))
    lengths = draw_lengths(jax.random.fold_in(seeds[5], 71), 0)
    return dict(grads_out=grads_out, inputs=inputs, basis_out=basis_out, basis_in=basis_in, lengths=lengths)


def reference(grads_out, inputs, basis_out, basis_in, lengths):
    positions = jnp.arange(LEN).astype(jnp.int32)
    live = (positions[None, :] < lengths[:, None]).reshape(-1)
    masked = jnp.where(live[:, None], grads_out, jnp.zeros_like(grads_out))
    rotated = jnp.dot(masked, basis_out, preferred_element_type=jnp.float32).astype(jnp.bfloat16)
    panel = jnp.dot(inputs, basis_in, preferred_element_type=jnp.float32).astype(jnp.bfloat16)
    rotated_seq = rotated.reshape(SEQS, LEN, FW)
    panel_seq = panel.reshape(SEQS, LEN, DW)

    def accumulate(total, pair):
        left_factor, right_factor = pair
        sample_case = jnp.dot(left_factor.T, right_factor, preferred_element_type=jnp.float32)
        return total + sample_case * sample_case, None

    total, unused = lax.scan(accumulate, jnp.zeros((FW, DW), jnp.float32), (rotated_seq, panel_seq))
    return total / TOKENS
```

```python
import functools

import jax
import jax.numpy as jnp
from jax import lax
from jax.experimental import pallas as pl
from jax.experimental.pallas import tpu as pltpu
from jax.sharding import Mesh, PartitionSpec as P

BF = jnp.bfloat16
F32 = jnp.float32
DP = ("z", "x")
TN = ("y", "c")


def exchange(blocks, axis):
    return lax.all_to_all(blocks, axis, split_axis=0, concat_axis=0, tiled=True)


def gather(block, axis):
    count = lax.axis_size(axis)
    return exchange(jnp.broadcast_to(block[None], (count,) + block.shape), axis)


def example_kernel(groups, scale, left_ref, own_ref, other_ref, out_ref):
    rows = left_ref.shape[1]
    lanes = left_ref.shape[2]
    columns = own_ref.shape[-1]
    per_group = lanes // 16
    slot = lax.broadcasted_iota(jnp.int32, (rows, 2 * lanes), 1)
    owner = (slot % lanes) // 16
    total = jnp.zeros((rows, columns), F32)
    for k in range(groups):
        left = jnp.concatenate([left_ref[k], left_ref[groups + k]], axis=1)
        right = jnp.concatenate([own_ref[k], other_ref[k]], axis=0)
        for j in range(per_group):
            picked = jnp.where(owner == j, left, jnp.zeros_like(left))
            one = jnp.dot(picked, right, preferred_element_type=F32)
            total = total + one * one
    total = total * scale
    for q in range(out_ref.shape[0]):
        out_ref[q] = total[:, q * out_ref.shape[2] : (q + 1) * out_ref.shape[2]]


def examples(left, own, other, parts, scale):
    blocks, rows, lanes = left.shape
    columns = own.shape[-1]
    groups = blocks // 2
    return pl.pallas_call(
        functools.partial(example_kernel, groups, scale),
        out_shape=jax.ShapeDtypeStruct((parts, rows, columns // parts), F32),
        compiler_params=pltpu.CompilerParams(vmem_limit_bytes=40 * 1024 * 1024),
        cost_estimate=pl.CostEstimate(
            flops=2 * 32 * 32 * rows * columns, bytes_accessed=2_000_000, transcendentals=0
        ),
    )(left, own, other)


def per_device(grads_out, inputs, basis_out, basis_in, lengths):
    nz, nx, ny, nc = (lax.axis_size(a) for a in ("z", "x", "y", "c"))
    ndp, nt = nz * nx, ny * nc
    core = lax.axis_index("c")
    tensor = lax.axis_index("y") * nc + core
    slots = grads_out.shape[0]
    half = slots // nc
    wide = basis_out.shape[0]
    cols = basis_out.shape[1]

    width_in = basis_in.shape[0]
    slab = lax.dynamic_slice_in_dim(inputs, tensor * width_in, width_in, 1)
    with jax.named_scope("slab_z"):
        slab_z = gather(slab, "z").reshape(nz * slots, width_in)
    with jax.named_scope("basis_x"):
        basis_x = gather(basis_in, "x")

    rows = lax.dynamic_slice_in_dim(grads_out, core * half, half, 0)
    live = (core * half + jnp.arange(half))[:, None] < lengths[0]
    rows = jnp.where(live, rows, jnp.zeros_like(rows))
    blocks = rows.reshape(half, ndp, wide).transpose(1, 0, 2)
    with jax.named_scope("rows_dp"):
        own = exchange(blocks, DP).reshape(ndp * half, wide)
    with jax.named_scope("rows_c"):
        other = lax.ppermute(own, "c", [(0, 1), (1, 0)])

    def rotate(tokens):
        part = lax.dot_general(
            basis_out, tokens, (((0,), (1,)), ((), ())), preferred_element_type=F32
        ).astype(BF)
        part = part.reshape(nx, cols // nx, nz // 2, 128)
        return part.transpose(2, 0, 1, 3)

    parts = jnp.concatenate([rotate(own), rotate(other)], axis=0)
    parts = parts.reshape(ndp, cols // nx, 128)
    with jax.named_scope("sum_dp"):
        parts = exchange(parts, DP)
    rotated = jnp.sum(parts.astype(F32), axis=0).astype(BF)
    with jax.named_scope("rotated_z"):
        rotated = gather(rotated, "z")

    partial_in = lax.dot_general(
        slab_z, basis_x, (((1,), (1,)), ((), ())), preferred_element_type=F32
    ).astype(BF)
    columns = nx * basis_in.shape[1]
    partial_in = partial_in.reshape(nt, nz * slots // nt, columns)
    with jax.named_scope("panel_sum"):
        partial_in = exchange(partial_in, TN)
    piece = jnp.sum(partial_in.astype(F32), axis=0).astype(BF)
    with jax.named_scope("panel_x"):
        piece = gather(piece, "x")
    with jax.named_scope("panel_T"):
        panel = gather(piece, TN)
    panel = panel.reshape(nz, 2, nx, half, columns).transpose(1, 0, 2, 3, 4)
    panel = panel.reshape(2, nz // 2, 128, columns)
    first = lax.dynamic_index_in_dim(panel, core, 0, keepdims=False)
    second = lax.dynamic_index_in_dim(panel, 1 - core, 0, keepdims=False)

    result = examples(rotated, first, second, nx, 1.0 / (ndp * slots))
    with jax.named_scope("out_x"):
        result = exchange(result, "x")
    return result.reshape(cols, result.shape[2])


def solution(mesh):
    fine = Mesh(mesh.devices.reshape(8, 4, 8, 2), ("z", "x", "y", "c"))
    placed = (P(DP, None), P(DP, None), P(DP, TN), P(TN, DP), P(DP))
    return jax.shard_map(
        per_device, mesh=fine, in_specs=placed, out_specs=P(TN, DP), check_vma=False
    )
```

```python
import functools

import jax
import jax.numpy as jnp
from jax import lax
from jax.experimental import pallas as pl
from jax.experimental.pallas import tpu as pltpu
from jax.sharding import Mesh, PartitionSpec as P

BF = jnp.bfloat16
F32 = jnp.float32
DP = ("z", "x")
TN = ("y", "c")
MIB = 1024 * 1024
PARAMS = pltpu.CompilerParams(vmem_limit_bytes=40 * MIB)
SMEM = pltpu.SMEM
VMEM = pltpu.VMEM


def exchange(blocks, axis):
    return lax.all_to_all(blocks, axis, split_axis=0, concat_axis=0, tiled=True)


def swap(block, axis, bit):
    count = lax.axis_size(axis)
    return lax.ppermute(block, axis, [(i, i ^ bit) for i in range(count)])


def bits(axis):
    count = lax.axis_size(axis)
    return [1 << k for k in range(count.bit_length() - 1)]


def double(block, axis):
    for bit in bits(axis):
        block = jnp.concatenate([block, swap(block, axis, bit)], axis=0)
    return block


def halve(block, axis):
    index = lax.axis_index(axis)
    for bit in reversed(bits(axis)):
        upper = (index // bit) % 2
        kept = lax.dynamic_slice_in_dim(block, upper * bit, bit, 0)
        sent = lax.dynamic_slice_in_dim(block, (1 - upper) * bit, bit, 0)
        block = kept + swap(sent, axis, bit)
    return block


def cost(flops, moved):
    return pl.CostEstimate(flops=flops, bytes_accessed=moved, transcendentals=0)


def split_kernel(half, at_ref, grads_ref, out_ref):
    parts, _, wide = out_ref.shape
    slot = at_ref[0] * half + lax.broadcasted_iota(jnp.int32, (half, wide), 0)
    live = slot < at_ref[1]
    for q in range(parts):
        piece = grads_ref[:, q * wide : (q + 1) * wide]
        out_ref[q] = jnp.where(live, piece, jnp.zeros_like(piece))


def split_rows(grads, at, half, parts, steps=4):
    wide = grads.shape[1] // parts
    each = parts // steps
    return pl.pallas_call(
        functools.partial(split_kernel, half),
        out_shape=jax.ShapeDtypeStruct((parts, half, wide), grads.dtype),
        grid_spec=pltpu.PrefetchScalarGridSpec(
            num_scalar_prefetch=1,
            grid=(steps,),
            in_specs=[pl.BlockSpec((half, each * wide), lambda i, at: (at[0], i))],
            out_specs=pl.BlockSpec((each, half, wide), lambda i, at: (i, 0, 0)),
        ),
        compiler_params=PARAMS,
        cost_estimate=cost(0, 4 * half * grads.shape[1]),
    )(at, grads)


def rotate_kernel(tokens_ref, basis_ref, *rest):
    out_ref = rest[-1]
    product = jnp.dot(tokens_ref[...], basis_ref[...], preferred_element_type=F32)
    lanes = out_ref.shape[2]
    rows = out_ref.shape[1]
    groups = product.shape[0] // lanes
    pieces = product.shape[1] // rows
    for g in range(groups):
        turned = product[g * lanes : (g + 1) * lanes].T.astype(BF)
        for q in range(pieces):
            out_ref[g * pieces + q] = turned[q * rows : (q + 1) * rows]


def rotate(tokens, basis, place, pieces, before=None):
    count, wide = tokens.shape
    columns = basis.shape[1]
    rows = columns // pieces
    blocks = pieces * count // 128
    in_specs = [
        pl.BlockSpec((count, wide), lambda i: (0, 0)),
        pl.BlockSpec((wide, columns), lambda i: (0, 0)),
    ]
    args = [tokens, basis]
    aliases = {}
    if before is not None:
        in_specs.append(pl.BlockSpec(memory_space=pl.ANY))
        args.append(before)
        aliases = {2: 0}
    return pl.pallas_call(
        rotate_kernel,
        out_shape=jax.ShapeDtypeStruct((2 * blocks, rows, 128), BF),
        grid=(1,),
        in_specs=in_specs,
        out_specs=pl.BlockSpec((blocks, rows, 128), lambda i: (place, 0, 0)),
        input_output_aliases=aliases,
        compiler_params=PARAMS,
        cost_estimate=cost(2 * count * wide * columns, 2 * count * (wide + columns)),
    )(*args)


def sum_kernel(parts_ref, out_ref):
    total = parts_ref[0].astype(F32)
    for q in range(1, parts_ref.shape[0]):
        total = total + parts_ref[q].astype(F32)
    total = total.astype(BF)
    for q in range(out_ref.shape[0]):
        out_ref[q] = total


def sum_parts(parts, copies, steps=2):
    count, rows, lanes = parts.shape
    return pl.pallas_call(
        sum_kernel,
        out_shape=jax.ShapeDtypeStruct((copies, rows, lanes), BF),
        grid=(steps,),
        in_specs=[pl.BlockSpec((count, rows // steps, lanes), lambda i: (0, i, 0))],
        out_specs=pl.BlockSpec((copies, rows // steps, lanes), lambda i: (0, i, 0)),
        compiler_params=PARAMS,
        cost_estimate=cost(parts.size, 2 * parts.size),
    )(parts)


def panel_kernel(at_ref, slab_ref, basis_ref, out_ref):
    cores, count, slots, deep = slab_ref.shape
    for q in range(basis_ref.shape[1]):
        total = jnp.zeros((count * slots, basis_ref.shape[3]), F32)
        for r in range(cores):
            left = slab_ref[r].reshape(count * slots, deep)
            right = basis_ref[r, q ^ at_ref[0]]
            total = total + jnp.dot(left, right, preferred_element_type=F32)
        lanes = total.shape[1]
        out_ref[:, :, q * lanes : (q + 1) * lanes] = total.reshape(count, slots, lanes)


def panel_part(at, slab, basis):
    cores, count, slots, deep = slab.shape
    columns = basis.shape[1] * basis.shape[3]
    return pl.pallas_call(
        panel_kernel,
        out_shape=jax.ShapeDtypeStruct((count, slots, columns), F32),
        in_specs=[pl.BlockSpec(memory_space=SMEM)] + [pl.BlockSpec(memory_space=VMEM)] * 2,
        out_specs=pl.BlockSpec(memory_space=VMEM),
        compiler_params=PARAMS,
        cost_estimate=cost(2 * count * slots * columns * deep * cores, 2 * basis.size),
    )(at, slab, basis)


def example_kernel(nx, scale, at_ref, left_ref, own_ref, other_ref, out_ref):
    blocks, rows, lanes = left_ref.shape
    slots, columns = own_ref.shape[2:]
    groups = blocks // 2
    per_group = lanes // slots
    slot = lax.broadcasted_iota(jnp.int32, (rows, 2 * lanes), 1)
    owner = (slot % lanes) // slots
    total = jnp.zeros((rows, columns), F32)
    for k in range(groups):
        left = jnp.concatenate([left_ref[k], left_ref[groups + k]], axis=1)
        places = [divmod(k * per_group + j, nx) for j in range(per_group)]
        places = [(xp ^ at_ref[0], zp ^ at_ref[1]) for zp, xp in places]
        right = jnp.concatenate(
            [own_ref[a, b] for a, b in places] + [other_ref[a, b] for a, b in places], axis=0
        )
        for j in range(per_group):
            picked = jnp.where(owner == j, left, jnp.zeros_like(left))
            one = jnp.dot(picked, right, preferred_element_type=F32)
            total = total + one * one
    total = total * scale
    wide = out_ref.shape[2]
    for q in range(out_ref.shape[0]):
        out_ref[q] = total[:, q * wide : (q + 1) * wide]


def examples(at, left, own, other, nx, scale):
    blocks, rows, lanes = left.shape
    columns = own.shape[-1]
    return pl.pallas_call(
        functools.partial(example_kernel, nx, scale),
        out_shape=jax.ShapeDtypeStruct((nx, rows, columns // nx), F32),
        in_specs=[pl.BlockSpec(memory_space=SMEM)] + [pl.BlockSpec(memory_space=VMEM)] * 3,
        out_specs=pl.BlockSpec(memory_space=VMEM),
        compiler_params=PARAMS,
        cost_estimate=cost(2 * blocks * lanes * rows * columns, 4 * own.size),
    )(at, left, own, other)


def per_device(grads_out, inputs, basis_out, basis_in, lengths):
    nz, nx, ny, nc = (lax.axis_size(a) for a in ("z", "x", "y", "c"))
    iz, ix, iy, ic = (lax.axis_index(a) for a in ("z", "x", "y", "c"))
    slots = grads_out.shape[0]
    half = slots // nc
    wide, columns = basis_out.shape
    deep = basis_in.shape[0]
    at = jnp.stack([ix, iz ^ iy]).astype(jnp.int32)

    blocks = split_rows(grads_out, jnp.stack([ic.astype(jnp.int32), lengths[0]]), half, nz * nx)
    with jax.named_scope("rows_dp"):
        own = exchange(blocks, DP).reshape(nz * nx * half, wide)

    with jax.named_scope("slab_z"):
        mine = lax.dynamic_slice(inputs, (ic * half, (iy * nc + ic) * deep), (half, deep))
        theirs = lax.dynamic_slice(inputs, (ic * half, (iy * nc + 1 - ic) * deep), (half, deep))
        slab = jnp.stack([mine, theirs])[:, None]
        for bit in bits("z"):
            slab = jnp.concatenate([slab, swap(slab, "z", bit)], axis=1)
    with jax.named_scope("basis_xc"):
        basis_x = double(basis_in[None], "x")
        basis_x = jnp.stack([basis_x, swap(basis_x, "c", 1)])
    own, slab, basis_x = lax.optimization_barrier((own, slab, basis_x))
    part_in = panel_part(at, slab, basis_x)
    with jax.named_scope("panel_sum"):
        piece = halve(part_in, "y").astype(BF)
    with jax.named_scope("panel_y"):
        piece = double(piece, "y")
    with jax.named_scope("panel_x"):
        piece = double(piece[None], "x")
    with jax.named_scope("panel_c"):
        piece_other = swap(piece, "c", 1)

    with jax.named_scope("rows_c"):
        other = swap(own, "c", 1)
    parts = rotate(own, basis_out, 0, nx)
    parts = rotate(other, basis_out, 1, nx, parts)
    with jax.named_scope("sum_dp"):
        parts = exchange(parts, DP)
    rotated = sum_parts(parts, nz)
    with jax.named_scope("rotated_z"):
        rotated = exchange(rotated, "z")

    result = examples(at, rotated, piece, piece_other, nx, 1.0 / (nz * nx * slots))
    with jax.named_scope("out_x"):
        result = exchange(result, "x")
    return result.reshape(columns, result.shape[2])


def solution(mesh):
    fine = Mesh(mesh.devices.reshape(8, 4, 8, 2), ("z", "x", "y", "c"))
    placed = (P(DP, None), P(DP, None), P(DP, TN), P(TN, DP), P(DP))
    return jax.shard_map(
        per_device, mesh=fine, in_specs=placed, out_specs=P(TN, DP), check_vma=False
    )
```

```python
import functools

import jax
import jax.numpy as jnp
from jax import lax
from jax.experimental import pallas as pl
from jax.experimental.pallas import tpu as pltpu
from jax.sharding import Mesh, PartitionSpec as P

BF = jnp.bfloat16
F32 = jnp.float32
DP = ("z", "x")
TN = ("y", "c")
MIB = 1024 * 1024
PARAMS = pltpu.CompilerParams(vmem_limit_bytes=40 * MIB)
SMEM = pltpu.SMEM
VMEM = pltpu.VMEM


def exchange(blocks, axis):
    return lax.all_to_all(blocks, axis, split_axis=0, concat_axis=0, tiled=True)


def swap(block, axis, bit):
    count = lax.axis_size(axis)
    return lax.ppermute(block, axis, [(i, i ^ bit) for i in range(count)])


def bits(axis):
    count = lax.axis_size(axis)
    return [1 << k for k in reversed(range(count.bit_length() - 1))]


def reverse(index, width):
    result = 0
    for k in range(width):
        result = result | (((index >> k) & 1) << (width - 1 - k))
    return result


def double(block, axis):
    for bit in bits(axis):
        block = jnp.concatenate([block, swap(block, axis, bit)], axis=0)
    return block


def total_over(block, axis):
    for bit in reversed(bits(axis)):
        block = block + swap(block.astype(BF), axis, bit).astype(F32)
    return block


def cost(flops, moved):
    return pl.CostEstimate(flops=flops, bytes_accessed=moved, transcendentals=0)


def split_kernel(half, at_ref, grads_ref, out_ref):
    parts, _, wide = out_ref.shape
    slot = at_ref[0] * half + lax.broadcasted_iota(jnp.int32, (half, wide), 0)
    live = slot < at_ref[1]
    for q in range(parts):
        piece = grads_ref[:, q * wide : (q + 1) * wide]
        out_ref[q] = jnp.where(live, piece, jnp.zeros_like(piece))


def split_rows(grads, at, half, parts, steps=4):
    wide = grads.shape[1] // parts
    each = parts // steps
    return pl.pallas_call(
        functools.partial(split_kernel, half),
        out_shape=jax.ShapeDtypeStruct((parts, half, wide), grads.dtype),
        grid_spec=pltpu.PrefetchScalarGridSpec(
            num_scalar_prefetch=1,
            grid=(steps,),
            in_specs=[pl.BlockSpec((half, each * wide), lambda i, at: (at[0], i))],
            out_specs=pl.BlockSpec((each, half, wide), lambda i, at: (i, 0, 0)),
        ),
        compiler_params=pltpu.CompilerParams(vmem_limit_bytes=58 * MIB),
        cost_estimate=cost(0, 4 * half * grads.shape[1]),
    )(at, grads)


def rotate_kernel(tokens_ref, basis_ref, *rest):
    out_ref = rest[-1]
    product = jnp.dot(tokens_ref[...], basis_ref[...], preferred_element_type=F32)
    lanes = out_ref.shape[2]
    rows = out_ref.shape[1]
    groups = product.shape[0] // lanes
    pieces = product.shape[1] // rows
    for g in range(groups):
        turned = product[g * lanes : (g + 1) * lanes].T.astype(BF)
        for q in range(pieces):
            out_ref[g * pieces + q] = turned[q * rows : (q + 1) * rows]


def rotate(tokens, basis, place, pieces, before=None):
    count, wide = tokens.shape
    columns = basis.shape[1]
    rows = columns // pieces
    blocks = pieces * count // 128
    in_specs = [
        pl.BlockSpec((count, wide), lambda i: (0, 0)),
        pl.BlockSpec((wide, columns), lambda i: (0, 0)),
    ]
    args = [tokens, basis]
    aliases = {}
    if before is not None:
        in_specs.append(pl.BlockSpec(memory_space=pl.ANY))
        args.append(before)
        aliases = {2: 0}
    return pl.pallas_call(
        rotate_kernel,
        out_shape=jax.ShapeDtypeStruct((2 * blocks, rows, 128), BF),
        grid=(1,),
        in_specs=in_specs,
        out_specs=pl.BlockSpec((blocks, rows, 128), lambda i: (place, 0, 0)),
        input_output_aliases=aliases,
        compiler_params=PARAMS,
        cost_estimate=cost(2 * count * wide * columns, 2 * count * (wide + columns)),
    )(*args)


def sum_kernel(parts_ref, out_ref):
    total = parts_ref[0].astype(F32)
    for q in range(1, parts_ref.shape[0]):
        total = total + parts_ref[q].astype(F32)
    total = total.astype(BF)
    for q in range(out_ref.shape[0]):
        out_ref[q] = total


def sum_parts(parts, copies, steps=2):
    count, rows, lanes = parts.shape
    return pl.pallas_call(
        sum_kernel,
        out_shape=jax.ShapeDtypeStruct((copies, rows, lanes), BF),
        grid=(steps,),
        in_specs=[pl.BlockSpec((count, rows // steps, lanes), lambda i: (0, i, 0))],
        out_specs=pl.BlockSpec((copies, rows // steps, lanes), lambda i: (0, i, 0)),
        compiler_params=PARAMS,
        cost_estimate=cost(parts.size, 2 * parts.size),
    )(parts)


def panel_kernel(at_ref, slab_ref, basis_ref, out_ref):
    cores, count, slots, deep = slab_ref.shape
    for q in range(basis_ref.shape[1]):
        total = jnp.zeros((count * slots, basis_ref.shape[3]), F32)
        for r in range(cores):
            left = slab_ref[r].reshape(count * slots, deep)
            right = basis_ref[r, reverse(q ^ at_ref[0], 2)]
            total = total + jnp.dot(left, right, preferred_element_type=F32)
        lanes = total.shape[1]
        out_ref[:, :, q * lanes : (q + 1) * lanes] = total.reshape(count, slots, lanes)


def panel_part(at, slab, basis):
    cores, count, slots, deep = slab.shape
    columns = basis.shape[1] * basis.shape[3]
    return pl.pallas_call(
        panel_kernel,
        out_shape=jax.ShapeDtypeStruct((count, slots, columns), F32),
        in_specs=[pl.BlockSpec(memory_space=SMEM)] + [pl.BlockSpec(memory_space=VMEM)] * 2,
        out_specs=pl.BlockSpec(memory_space=VMEM),
        compiler_params=PARAMS,
        cost_estimate=cost(2 * count * slots * columns * deep * cores, 2 * basis.size),
    )(at, slab, basis)


def example_kernel(nx, scale, at_ref, left_ref, own_ref, other_ref, out_ref):
    blocks, rows, lanes = left_ref.shape
    slots, columns = own_ref.shape[2:]
    groups = blocks // 2
    per_group = lanes // slots
    slot = lax.broadcasted_iota(jnp.int32, (rows, 2 * lanes), 1)
    owner = (slot % lanes) // slots
    total = jnp.zeros((rows, columns), F32)
    for k in range(groups):
        left = jnp.concatenate([left_ref[k], left_ref[groups + k]], axis=1)
        places = [divmod(k * per_group + j, nx) for j in range(per_group)]
        places = [(reverse(xp ^ at_ref[0], 2), reverse(zp ^ at_ref[1], 3)) for zp, xp in places]
        right = jnp.concatenate(
            [own_ref[a, b] for a, b in places] + [other_ref[a, b] for a, b in places], axis=0
        )
        for j in range(per_group):
            picked = jnp.where(owner == j, left, jnp.zeros_like(left))
            one = jnp.dot(picked, right, preferred_element_type=F32)
            total = total + one * one
    total = total * scale
    wide = out_ref.shape[2]
    for q in range(out_ref.shape[0]):
        out_ref[q] = total[:, q * wide : (q + 1) * wide]


def examples(at, left, own, other, nx, scale):
    blocks, rows, lanes = left.shape
    columns = own.shape[-1]
    return pl.pallas_call(
        functools.partial(example_kernel, nx, scale),
        out_shape=jax.ShapeDtypeStruct((nx, rows, columns // nx), F32),
        in_specs=[pl.BlockSpec(memory_space=SMEM)] + [pl.BlockSpec(memory_space=VMEM)] * 3,
        out_specs=pl.BlockSpec(memory_space=VMEM),
        compiler_params=PARAMS,
        cost_estimate=cost(2 * blocks * lanes * rows * columns, 4 * own.size),
    )(at, left, own, other)


def per_device(grads_out, inputs, basis_out, basis_in, lengths):
    nz, nx, ny, nc = (lax.axis_size(a) for a in ("z", "x", "y", "c"))
    iz, ix, iy, ic = (lax.axis_index(a) for a in ("z", "x", "y", "c"))
    slots = grads_out.shape[0]
    half = slots // nc
    wide, columns = basis_out.shape
    deep = basis_in.shape[0]
    at = jnp.stack([ix, iz]).astype(jnp.int32)

    blocks = split_rows(grads_out, jnp.stack([ic.astype(jnp.int32), lengths[0]]), half, nz * nx)
    with jax.named_scope("rows_dp"):
        own = exchange(blocks, DP).reshape(nz * nx * half, wide)

    mine = lax.dynamic_slice(inputs, (ic * half, (iy * nc + ic) * deep), (half, deep))
    theirs = lax.dynamic_slice(inputs, (ic * half, (iy * nc + 1 - ic) * deep), (half, deep))
    slab = jnp.stack([mine, theirs])[:, None]
    basis_x = basis_in[None]
    with jax.named_scope("panel_gather"):
        for bit in bits("z"):
            more_slab = swap(slab, "z", bit)
            if bit > 1:
                more_basis = swap(basis_x, "x", bit // 2)
            else:
                more_basis = swap(basis_x, "c", 1)
            more_slab, more_basis = lax.optimization_barrier((more_slab, more_basis))
            slab = jnp.concatenate([slab, more_slab], axis=1)
            if bit > 1:
                basis_x = jnp.concatenate([basis_x, more_basis], axis=0)
            else:
                basis_x = jnp.stack([basis_x, more_basis])
    own, slab, basis_x = lax.optimization_barrier((own, slab, basis_x))
    part_in = panel_part(at, slab, basis_x)
    with jax.named_scope("panel_sum"):
        piece = total_over(part_in, "y").astype(BF)
    with jax.named_scope("panel_x"):
        piece = double(piece[None], "x")
    with jax.named_scope("panel_c"):
        piece_other = swap(piece, "c", 1)

    with jax.named_scope("rows_c"):
        other = swap(own, "c", 1)
    parts = rotate(own, basis_out, 0, nx)
    parts = rotate(other, basis_out, 1, nx, parts)
    with jax.named_scope("sum_dp"):
        parts = exchange(parts, DP)
    rotated = sum_parts(parts, nz)
    with jax.named_scope("rotated_z"):
        rotated = exchange(rotated, "z")

    result = examples(at, rotated, piece, piece_other, nx, 1.0 / (nz * nx * slots))
    with jax.named_scope("out_x"):
        result = exchange(result, "x")
    return result.reshape(columns, result.shape[2])


def solution(mesh):
    fine = Mesh(mesh.devices.reshape(8, 4, 8, 2), ("z", "x", "y", "c"))
    placed = (P(DP, None), P(DP, None), P(DP, TN), P(TN, DP), P(DP))
    return jax.shard_map(
        per_device, mesh=fine, in_specs=placed, out_specs=P(TN, DP), check_vma=False
    )
```

```python
import functools

import jax
import jax.numpy as jnp
from jax import lax
from jax.experimental import pallas as pl
from jax.experimental.pallas import tpu as pltpu
from jax.sharding import Mesh, PartitionSpec as P

BF = jnp.bfloat16
F32 = jnp.float32
DP = ("z", "x")
TN = ("y", "c")
MIB = 1024 * 1024
PARAMS = pltpu.CompilerParams(vmem_limit_bytes=40 * MIB)
SMEM = pltpu.SMEM
VMEM = pltpu.VMEM


def exchange(blocks, axis):
    return lax.all_to_all(blocks, axis, split_axis=0, concat_axis=0, tiled=True)


def swap(block, axis, bit):
    count = lax.axis_size(axis)
    return lax.ppermute(block, axis, [(i, i ^ bit) for i in range(count)])


def bits(axis):
    count = lax.axis_size(axis)
    return [1 << k for k in reversed(range(count.bit_length() - 1))]


def reverse(index, width):
    result = 0
    for k in range(width):
        result = result | (((index >> k) & 1) << (width - 1 - k))
    return result


def double(block, axis):
    for bit in bits(axis):
        block = jnp.concatenate([block, swap(block, axis, bit)], axis=0)
    return block


def add_from(block, axis, bit):
    return block + swap(block.astype(BF), axis, bit).astype(F32)


def cost(flops, moved):
    return pl.CostEstimate(flops=flops, bytes_accessed=moved, transcendentals=0)


def split_kernel(length_ref, grads_ref, out_ref, held, sems):
    parts, half, wide = out_ref.shape
    steps, _, chunk = held.shape
    each = parts // steps
    first = lax.axis_index("c") * half
    copies = [
        pltpu.make_async_copy(
            grads_ref.at[pl.ds(first, half), pl.ds(k * chunk, chunk)], held.at[k], sems.at[k]
        )
        for k in range(steps)
    ]
    for copy in copies:
        copy.start()
    slot = first + lax.broadcasted_iota(jnp.int32, (half, wide), 0)
    live = slot < length_ref[0]
    for k in range(steps):
        copies[k].wait()
        for q in range(each):
            piece = held[k, :, q * wide : (q + 1) * wide]
            out_ref[k * each + q] = jnp.where(live, piece, jnp.zeros_like(piece))


def split_rows(grads, length, half, parts, steps=4):
    wide = grads.shape[1] // parts
    return pl.pallas_call(
        split_kernel,
        out_shape=jax.ShapeDtypeStruct((parts, half, wide), grads.dtype),
        in_specs=[pl.BlockSpec(memory_space=SMEM), pl.BlockSpec(memory_space=pl.ANY)],
        out_specs=pl.BlockSpec(memory_space=VMEM),
        scratch_shapes=[
            VMEM((steps, half, grads.shape[1] // steps), grads.dtype),
            pltpu.SemaphoreType.DMA((steps,)),
        ],
        compiler_params=pltpu.CompilerParams(vmem_limit_bytes=58 * MIB),
        cost_estimate=cost(0, 4 * half * grads.shape[1]),
    )(length, grads)


def rotate_kernel(tokens_ref, basis_ref, *rest):
    out_ref = rest[-1]
    product = jnp.dot(tokens_ref[...], basis_ref[...], preferred_element_type=F32)
    pieces, rows, count = out_ref.shape
    for g in range(0, count, 128):
        turned = product[g : g + 128].T.astype(BF)
        for q in range(pieces):
            out_ref[q, :, g : g + 128] = turned[q * rows : (q + 1) * rows]


def rotate(tokens, basis, place, pieces, before=None):
    count, wide = tokens.shape
    columns = basis.shape[1]
    rows = columns // pieces
    in_specs = [
        pl.BlockSpec((count, wide), lambda i: (0, 0)),
        pl.BlockSpec((wide, columns), lambda i: (0, 0)),
    ]
    args = [tokens, basis]
    aliases = {}
    if before is not None:
        in_specs.append(pl.BlockSpec(memory_space=pl.ANY))
        args.append(before)
        aliases = {2: 0}
    return pl.pallas_call(
        rotate_kernel,
        out_shape=jax.ShapeDtypeStruct((pieces, rows, 2 * count), BF),
        grid=(1,),
        in_specs=in_specs,
        out_specs=pl.BlockSpec((pieces, rows, count), lambda i: (0, 0, place)),
        input_output_aliases=aliases,
        compiler_params=PARAMS,
        cost_estimate=cost(2 * count * wide * columns, 2 * count * (wide + columns)),
    )(*args)


def sum_lanes_kernel(parts_ref, out_ref):
    for g in range(out_ref.shape[0]):
        lanes = slice(g * 128, (g + 1) * 128)
        total = parts_ref[0, :, lanes].astype(F32)
        for q in range(1, parts_ref.shape[0]):
            total = total + parts_ref[q, :, lanes].astype(F32)
        out_ref[g] = total.astype(BF)


def sum_lanes(parts, steps=2):
    count, rows, lanes = parts.shape
    blocks = lanes // 128
    return pl.pallas_call(
        sum_lanes_kernel,
        out_shape=jax.ShapeDtypeStruct((blocks, rows, 128), BF),
        grid=(steps,),
        in_specs=[pl.BlockSpec((count, rows, lanes // steps), lambda i: (0, 0, i))],
        out_specs=pl.BlockSpec((blocks // steps, rows, 128), lambda i: (i, 0, 0)),
        compiler_params=PARAMS,
        cost_estimate=cost(parts.size, 2 * parts.size),
    )(parts)


def sum_kernel(parts_ref, out_ref):
    total = parts_ref[0].astype(F32)
    for q in range(1, parts_ref.shape[0]):
        total = total + parts_ref[q].astype(F32)
    total = total.astype(BF)
    for q in range(out_ref.shape[0]):
        out_ref[q] = total


def sum_parts(parts, copies, steps=2):
    count, rows, lanes = parts.shape
    return pl.pallas_call(
        sum_kernel,
        out_shape=jax.ShapeDtypeStruct((copies, rows, lanes), BF),
        grid=(steps,),
        in_specs=[pl.BlockSpec((count, rows // steps, lanes), lambda i: (0, i, 0))],
        out_specs=pl.BlockSpec((copies, rows // steps, lanes), lambda i: (0, i, 0)),
        compiler_params=PARAMS,
        cost_estimate=cost(parts.size, 2 * parts.size),
    )(parts)


def panel_kernel(at_ref, slab_ref, basis_ref, out_ref):
    cores, count, slots, deep = slab_ref.shape
    for q in range(basis_ref.shape[1]):
        total = jnp.zeros((count * slots, basis_ref.shape[3]), F32)
        for r in range(cores):
            left = slab_ref[r].reshape(count * slots, deep)
            right = basis_ref[r, reverse(q ^ at_ref[0], 2)]
            total = total + jnp.dot(left, right, preferred_element_type=F32)
        lanes = total.shape[1]
        out_ref[:, :, q * lanes : (q + 1) * lanes] = total.reshape(count, slots, lanes)


def panel_part(at, slab, basis):
    cores, count, slots, deep = slab.shape
    columns = basis.shape[1] * basis.shape[3]
    return pl.pallas_call(
        panel_kernel,
        out_shape=jax.ShapeDtypeStruct((count, slots, columns), F32),
        in_specs=[pl.BlockSpec(memory_space=SMEM)] + [pl.BlockSpec(memory_space=VMEM)] * 2,
        out_specs=pl.BlockSpec(memory_space=VMEM),
        compiler_params=PARAMS,
        cost_estimate=cost(2 * count * slots * columns * deep * cores, 2 * basis.size),
    )(at, slab, basis)


def example_kernel(nx, scale, at_ref, left_ref, own_ref, other_ref, out_ref):
    blocks, rows, lanes = left_ref.shape
    slots, columns = own_ref.shape[2:]
    groups = blocks // 2
    per_group = lanes // slots
    slot = lax.broadcasted_iota(jnp.int32, (rows, 2 * lanes), 1)
    owner = (slot % lanes) // slots
    total = jnp.zeros((rows, columns), F32)
    for k in range(groups):
        left = jnp.concatenate([left_ref[k], left_ref[groups + k]], axis=1)
        places = [divmod(k * per_group + j, nx) for j in range(per_group)]
        places = [(xp ^ at_ref[0], reverse(zp ^ at_ref[1], 3)) for zp, xp in places]
        right = jnp.concatenate(
            [own_ref[a, b] for a, b in places] + [other_ref[a, b] for a, b in places], axis=0
        )
        for j in range(per_group):
            picked = jnp.where(owner == j, left, jnp.zeros_like(left))
            one = jnp.dot(picked, right, preferred_element_type=F32)
            total = total + one * one
    total = total * scale
    wide = out_ref.shape[2]
    for q in range(out_ref.shape[0]):
        out_ref[q] = total[:, q * wide : (q + 1) * wide]


def examples(at, left, own, other, nx, scale):
    blocks, rows, lanes = left.shape
    columns = own.shape[-1]
    return pl.pallas_call(
        functools.partial(example_kernel, nx, scale),
        out_shape=jax.ShapeDtypeStruct((nx, rows, columns // nx), F32),
        in_specs=[pl.BlockSpec(memory_space=SMEM)] + [pl.BlockSpec(memory_space=VMEM)] * 3,
        out_specs=pl.BlockSpec(memory_space=VMEM),
        compiler_params=PARAMS,
        cost_estimate=cost(2 * blocks * lanes * rows * columns, 4 * own.size),
    )(at, left, own, other)


def per_device(grads_out, inputs, basis_out, basis_in, lengths):
    nz, nx, ny, nc = (lax.axis_size(a) for a in ("z", "x", "y", "c"))
    iz, ix, iy, ic = (lax.axis_index(a) for a in ("z", "x", "y", "c"))
    slots = grads_out.shape[0]
    half = slots // nc
    wide, columns = basis_out.shape
    deep = basis_in.shape[0]
    at = jnp.stack([ix, iz]).astype(jnp.int32)
    tie = lax.optimization_barrier

    blocks = split_rows(grads_out, lengths, half, nz * nx)
    with jax.named_scope("rows_dp"):
        own = exchange(blocks, DP).reshape(nz * nx * half, wide)

    mine = lax.dynamic_slice(inputs, (ic * half, (iy * nc + ic) * deep), (half, deep))
    theirs = lax.dynamic_slice(inputs, (ic * half, (iy * nc + 1 - ic) * deep), (half, deep))
    slab = jnp.stack([mine, theirs])[:, None]
    basis_x = basis_in[None]
    with jax.named_scope("panel_gather"):
        more_slab = swap(slab, "z", 4)
        basis_x = double(basis_x, "x")
        basis_x = jnp.stack([basis_x, swap(basis_x, "c", 1)])
        own, more_slab, basis_x = tie((own, more_slab, basis_x))
        slab = jnp.concatenate([slab, more_slab], axis=1)
        more_slab = swap(slab, "z", 2)

    with jax.named_scope("rows_c"):
        other = swap(own, "c", 1)
    parts = rotate(own, basis_out, 0, nx)
    other, more_slab = tie((other, more_slab))
    parts = rotate(other, basis_out, 1, nx, parts)
    with jax.named_scope("sum_x"):
        parts = exchange(parts, "x")

    with jax.named_scope("panel_gather"):
        slab = jnp.concatenate([slab, more_slab], axis=1)
        slab = jnp.concatenate([slab, swap(slab, "z", 1)], axis=1)
    piece = panel_part(at, slab, basis_x)
    with jax.named_scope("panel_sum"):
        piece = add_from(piece, "y", 1)
        piece = add_from(piece, "y", 2)
    parts, piece = tie((parts, piece))
    parts = sum_lanes(parts)
    with jax.named_scope("sum_z"):
        parts = exchange(parts, "z")
    with jax.named_scope("panel_sum"):
        piece = add_from(piece, "y", 4).astype(BF)
    rotated = sum_parts(parts, nz)
    with jax.named_scope("rotated_z"):
        rotated = exchange(rotated, "z")
    with jax.named_scope("panel_x"):
        piece = jnp.stack([piece] + [swap(piece, "x", k) for k in range(1, 4)])
    with jax.named_scope("panel_c"):
        piece_other = swap(piece, "c", 1)

    result = examples(at, rotated, piece, piece_other, nx, 1.0 / (nz * nx * slots))
    with jax.named_scope("out_x"):
        result = exchange(result, "x")
    return result.reshape(columns, result.shape[2])


def solution(mesh):
    fine = Mesh(mesh.devices.reshape(8, 4, 8, 2), ("z", "x", "y", "c"))
    placed = (P(DP, None), P(DP, None), P(DP, TN), P(TN, DP), P(DP))
    return jax.shard_map(
        per_device, mesh=fine, in_specs=placed, out_specs=P(TN, DP), check_vma=False
    )
```

```python
import functools

import jax
import jax.numpy as jnp
from jax import lax
from jax.experimental import pallas as pl
from jax.experimental.pallas import tpu as pltpu
from jax.sharding import Mesh, PartitionSpec as P

BF = jnp.bfloat16
F32 = jnp.float32
DP = ("z", "x")
TN = ("y", "c")
MIB = 1024 * 1024
PARAMS = pltpu.CompilerParams(vmem_limit_bytes=40 * MIB)
SMEM = pltpu.SMEM
VMEM = pltpu.VMEM


def exchange(blocks, axis):
    return lax.all_to_all(blocks, axis, split_axis=0, concat_axis=0, tiled=True)


def swap(block, axis, bit):
    count = lax.axis_size(axis)
    return lax.ppermute(block, axis, [(i, i ^ bit) for i in range(count)])


def reverse(index, width):
    result = 0
    for k in range(width):
        result = result | (((index >> k) & 1) << (width - 1 - k))
    return result


def direct(block, axis):
    count = lax.axis_size(axis)
    return jnp.stack([block] + [swap(block, axis, k) for k in range(1, count)])


def add_from(block, axis, bit):
    return block + swap(block.astype(BF), axis, bit).astype(F32)


def cost(flops, moved):
    return pl.CostEstimate(flops=flops, bytes_accessed=moved, transcendentals=0)


def split_kernel(length_ref, grads_ref, out_ref, held, sems):
    parts, half, wide = out_ref.shape
    steps, _, chunk = held.shape
    each = parts // steps
    first = lax.axis_index("c") * half
    copies = [
        pltpu.make_async_copy(
            grads_ref.at[pl.ds(first, half), pl.ds(k * chunk, chunk)], held.at[k], sems.at[k]
        )
        for k in range(steps)
    ]
    for copy in copies:
        copy.start()
    slot = first + lax.broadcasted_iota(jnp.int32, (half, wide), 0)
    live = slot < length_ref[0]
    for k in range(steps):
        copies[k].wait()
        for q in range(each):
            piece = held[k, :, q * wide : (q + 1) * wide]
            out_ref[k * each + q] = jnp.where(live, piece, jnp.zeros_like(piece))


def split_rows(grads, length, half, parts, steps=4):
    wide = grads.shape[1] // parts
    return pl.pallas_call(
        split_kernel,
        out_shape=jax.ShapeDtypeStruct((parts, half, wide), grads.dtype),
        in_specs=[pl.BlockSpec(memory_space=SMEM), pl.BlockSpec(memory_space=pl.ANY)],
        out_specs=pl.BlockSpec(memory_space=VMEM),
        scratch_shapes=[
            VMEM((steps, half, grads.shape[1] // steps), grads.dtype),
            pltpu.SemaphoreType.DMA((steps,)),
        ],
        compiler_params=pltpu.CompilerParams(vmem_limit_bytes=58 * MIB),
        cost_estimate=cost(0, 4 * half * grads.shape[1]),
    )(length, grads)


def rotate_kernel(tokens_ref, basis_ref, *rest):
    out_ref = rest[-1]
    product = jnp.dot(tokens_ref[...], basis_ref[...], preferred_element_type=F32)
    pieces, rows, count = out_ref.shape
    for g in range(0, count, 128):
        turned = product[g : g + 128].T.astype(BF)
        for q in range(pieces):
            out_ref[q, :, g : g + 128] = turned[q * rows : (q + 1) * rows]


def rotate(tokens, basis, place, pieces, before=None):
    count, wide = tokens.shape
    columns = basis.shape[1]
    rows = columns // pieces
    in_specs = [
        pl.BlockSpec((count, wide), lambda i: (0, 0)),
        pl.BlockSpec((wide, columns), lambda i: (0, 0)),
    ]
    args = [tokens, basis]
    aliases = {}
    if before is not None:
        in_specs.append(pl.BlockSpec(memory_space=pl.ANY))
        args.append(before)
        aliases = {2: 0}
    return pl.pallas_call(
        rotate_kernel,
        out_shape=jax.ShapeDtypeStruct((pieces, rows, 2 * count), BF),
        grid=(1,),
        in_specs=in_specs,
        out_specs=pl.BlockSpec((pieces, rows, count), lambda i: (0, 0, place)),
        input_output_aliases=aliases,
        compiler_params=PARAMS,
        cost_estimate=cost(2 * count * wide * columns, 2 * count * (wide + columns)),
    )(*args)


def sum_lanes_kernel(parts_ref, out_ref):
    for g in range(out_ref.shape[0]):
        lanes = slice(g * 128, (g + 1) * 128)
        total = parts_ref[0, :, lanes].astype(F32)
        for q in range(1, parts_ref.shape[0]):
            total = total + parts_ref[q, :, lanes].astype(F32)
        out_ref[g] = total.astype(BF)


def sum_lanes(parts, steps=2):
    count, rows, lanes = parts.shape
    blocks = lanes // 128
    return pl.pallas_call(
        sum_lanes_kernel,
        out_shape=jax.ShapeDtypeStruct((blocks, rows, 128), BF),
        grid=(steps,),
        in_specs=[pl.BlockSpec((count, rows, lanes // steps), lambda i: (0, 0, i))],
        out_specs=pl.BlockSpec((blocks // steps, rows, 128), lambda i: (i, 0, 0)),
        compiler_params=PARAMS,
        cost_estimate=cost(parts.size, 2 * parts.size),
    )(parts)


def sum_kernel(parts_ref, out_ref):
    total = parts_ref[0].astype(F32)
    for q in range(1, parts_ref.shape[0]):
        total = total + parts_ref[q].astype(F32)
    total = total.astype(BF)
    for q in range(out_ref.shape[0]):
        out_ref[q] = total


def sum_parts(parts, copies, steps=2):
    count, rows, lanes = parts.shape
    return pl.pallas_call(
        sum_kernel,
        out_shape=jax.ShapeDtypeStruct((copies, rows, lanes), BF),
        grid=(steps,),
        in_specs=[pl.BlockSpec((count, rows // steps, lanes), lambda i: (0, i, 0))],
        out_specs=pl.BlockSpec((copies, rows // steps, lanes), lambda i: (0, i, 0)),
        compiler_params=PARAMS,
        cost_estimate=cost(parts.size, 2 * parts.size),
    )(parts)


def panel_kernel(at_ref, slab_ref, basis_ref, out_ref):
    cores, nx, chips, _, lanes = basis_ref.shape
    count, slots, _ = out_ref.shape
    for q in range(nx):
        total = jnp.zeros((count * slots, lanes), F32)
        for yr in range(chips):
            for cr in range(cores):
                left = slab_ref[yr * cores + cr]
                right = basis_ref[cr, q ^ at_ref[0], yr]
                total = total + jnp.dot(left, right, preferred_element_type=F32)
        out_ref[:, :, q * lanes : (q + 1) * lanes] = total.reshape(count, slots, lanes)


def panel_part(at, slab, basis):
    terms, count, slots, deep = slab.shape
    columns = basis.shape[1] * basis.shape[4]
    return pl.pallas_call(
        panel_kernel,
        out_shape=jax.ShapeDtypeStruct((count, slots, columns), F32),
        in_specs=[pl.BlockSpec(memory_space=SMEM)] + [pl.BlockSpec(memory_space=VMEM)] * 2,
        out_specs=pl.BlockSpec(memory_space=VMEM),
        compiler_params=PARAMS,
        cost_estimate=cost(2 * count * slots * columns * deep * terms, 2 * basis.size),
    )(at, slab.reshape(terms, count * slots, deep), basis)


def example_kernel(nx, scale, at_ref, left_ref, own_ref, other_ref, out_ref):
    blocks, rows, lanes = left_ref.shape
    slots, columns = own_ref.shape[2:]
    groups = blocks // 2
    per_group = lanes // slots
    slot = lax.broadcasted_iota(jnp.int32, (rows, 2 * lanes), 1)
    owner = (slot % lanes) // slots
    total = jnp.zeros((rows, columns), F32)
    for k in range(groups):
        left = jnp.concatenate([left_ref[k], left_ref[groups + k]], axis=1)
        places = [divmod(k * per_group + j, nx) for j in range(per_group)]
        places = [(xp ^ at_ref[0], reverse(zp ^ at_ref[1], 3)) for zp, xp in places]
        right = jnp.concatenate(
            [own_ref[a, b] for a, b in places] + [other_ref[a, b] for a, b in places], axis=0
        )
        for j in range(per_group):
            picked = jnp.where(owner == j, left, jnp.zeros_like(left))
            one = jnp.dot(picked, right, preferred_element_type=F32)
            total = total + one * one
    total = total * scale
    wide = out_ref.shape[2]
    for q in range(out_ref.shape[0]):
        out_ref[q] = total[:, q * wide : (q + 1) * wide]


def examples(at, left, own, other, nx, scale):
    blocks, rows, lanes = left.shape
    columns = own.shape[-1]
    return pl.pallas_call(
        functools.partial(example_kernel, nx, scale),
        out_shape=jax.ShapeDtypeStruct((nx, rows, columns // nx), F32),
        in_specs=[pl.BlockSpec(memory_space=SMEM)] + [pl.BlockSpec(memory_space=VMEM)] * 3,
        out_specs=pl.BlockSpec(memory_space=VMEM),
        compiler_params=PARAMS,
        cost_estimate=cost(2 * blocks * lanes * rows * columns, 4 * own.size),
    )(at, left, own, other)


def per_device(grads_out, inputs, basis_out, basis_in, lengths):
    nz, nx, ny, nc = (lax.axis_size(a) for a in ("z", "x", "y", "c"))
    iz, ix, iy, ic = (lax.axis_index(a) for a in ("z", "x", "y", "c"))
    slots = grads_out.shape[0]
    half = slots // nc
    wide, columns = basis_out.shape
    deep = basis_in.shape[0]
    at = jnp.stack([ix, iz]).astype(jnp.int32)
    tie = lax.optimization_barrier

    blocks = split_rows(grads_out, lengths, half, nz * nx)
    with jax.named_scope("rows_dp"):
        own = exchange(blocks, DP).reshape(nz * nx * half, wide)

    def features(yr, cr):
        start = ((iy ^ yr) * nc + (ic ^ cr)) * deep
        return lax.dynamic_slice(inputs, (ic * half, start), (half, deep))

    slab = jnp.stack([features(yr, cr) for yr in range(2) for cr in range(2)])[:, None]
    with jax.named_scope("basis_yxc"):
        basis_x = jnp.stack([basis_in, swap(basis_in, "y", 1)])
        basis_x = direct(basis_x, "x")
        own, basis_x, slab = tie((own, basis_x, slab))
        basis_x = jnp.stack([basis_x, swap(basis_x, "c", 1)])

    with jax.named_scope("rows_c"):
        other = swap(own, "c", 1)
    parts = rotate(own, basis_out, 0, nx)
    other, basis_x = tie((other, basis_x))
    parts = rotate(other, basis_out, 1, nx, parts)
    with jax.named_scope("sum_x"):
        parts = exchange(parts, "x")

    with jax.named_scope("slab_z"):
        for bit in (4, 2, 1):
            slab = jnp.concatenate([slab, swap(slab, "z", bit)], axis=1)
    piece = panel_part(at, slab, basis_x)
    parts, piece = tie((parts, piece))
    parts = sum_lanes(parts)
    with jax.named_scope("sum_z"):
        parts = exchange(parts, "z")
    with jax.named_scope("panel_sum"):
        piece = add_from(piece, "y", 2)
        piece = add_from(piece, "y", 4).astype(BF)
    rotated = sum_parts(parts, nz)
    with jax.named_scope("rotated_z"):
        rotated = exchange(rotated, "z")
    with jax.named_scope("panel_x"):
        piece = direct(piece, "x")
    with jax.named_scope("panel_c"):
        piece_other = swap(piece, "c", 1)

    result = examples(at, rotated, piece, piece_other, nx, 1.0 / (nz * nx * slots))
    with jax.named_scope("out_x"):
        result = exchange(result, "x")
    return result.reshape(columns, result.shape[2])


def solution(mesh):
    fine = Mesh(mesh.devices.reshape(8, 4, 8, 2), ("z", "x", "y", "c"))
    placed = (P(DP, None), P(DP, None), P(DP, TN), P(TN, DP), P(DP))
    return jax.shard_map(
        per_device, mesh=fine, in_specs=placed, out_specs=P(TN, DP), check_vma=False
    )
```

```python
import functools

import jax
import jax.numpy as jnp
from jax import lax
from jax.experimental import pallas as pl
from jax.experimental.pallas import tpu as pltpu
from jax.sharding import Mesh, PartitionSpec as P

BF = jnp.bfloat16
F32 = jnp.float32
DP = ("z", "x")
TN = ("y", "c")
MIB = 1024 * 1024
PARAMS = pltpu.CompilerParams(vmem_limit_bytes=40 * MIB)
SMEM = pltpu.SMEM
VMEM = pltpu.VMEM


def exchange(blocks, axis):
    return lax.all_to_all(blocks, axis, split_axis=0, concat_axis=0, tiled=True)


def swap(block, axis, bit):
    count = lax.axis_size(axis)
    return lax.ppermute(block, axis, [(i, i ^ bit) for i in range(count)])


def reverse(index, width):
    result = 0
    for k in range(width):
        result = result | (((index >> k) & 1) << (width - 1 - k))
    return result


def add_from(block, axis, bit):
    return block + swap(block.astype(BF), axis, bit).astype(F32)


def cost(flops, moved):
    return pl.CostEstimate(flops=flops, bytes_accessed=moved, transcendentals=0)


def split_kernel(length_ref, grads_ref, out_ref, held, sems):
    parts, half, wide = out_ref.shape
    steps, _, chunk = held.shape
    each = parts // steps
    first = lax.axis_index("c") * half
    copies = [
        pltpu.make_async_copy(
            grads_ref.at[pl.ds(first, half), pl.ds(k * chunk, chunk)], held.at[k], sems.at[k]
        )
        for k in range(steps)
    ]
    for copy in copies:
        copy.start()
    slot = first + lax.broadcasted_iota(jnp.int32, (half, wide), 0)
    live = slot < length_ref[0]
    for k in range(steps):
        copies[k].wait()
        for q in range(each):
            piece = held[k, :, q * wide : (q + 1) * wide]
            out_ref[k * each + q] = jnp.where(live, piece, jnp.zeros_like(piece))


def split_rows(grads, length, half, parts, steps=4):
    wide = grads.shape[1] // parts
    return pl.pallas_call(
        split_kernel,
        out_shape=jax.ShapeDtypeStruct((parts, half, wide), grads.dtype),
        in_specs=[pl.BlockSpec(memory_space=SMEM), pl.BlockSpec(memory_space=pl.ANY)],
        out_specs=pl.BlockSpec(memory_space=VMEM),
        scratch_shapes=[
            VMEM((steps, half, grads.shape[1] // steps), grads.dtype),
            pltpu.SemaphoreType.DMA((steps,)),
        ],
        compiler_params=pltpu.CompilerParams(vmem_limit_bytes=58 * MIB),
        cost_estimate=cost(0, 4 * half * grads.shape[1]),
    )(length, grads)


def rotate_kernel(tokens_ref, basis_ref, *rest):
    out_ref = rest[-1]
    product = jnp.dot(tokens_ref[...], basis_ref[...], preferred_element_type=F32)
    pieces, rows, count = out_ref.shape
    for g in range(0, count, 128):
        turned = product[g : g + 128].T.astype(BF)
        for q in range(pieces):
            out_ref[q, :, g : g + 128] = turned[q * rows : (q + 1) * rows]


def rotate(tokens, basis, place, pieces, before=None):
    count, wide = tokens.shape
    columns = basis.shape[1]
    rows = columns // pieces
    in_specs = [
        pl.BlockSpec((count, wide), lambda i: (0, 0)),
        pl.BlockSpec((wide, columns), lambda i: (0, 0)),
    ]
    args = [tokens, basis]
    aliases = {}
    if before is not None:
        in_specs.append(pl.BlockSpec(memory_space=pl.ANY))
        args.append(before)
        aliases = {2: 0}
    return pl.pallas_call(
        rotate_kernel,
        out_shape=jax.ShapeDtypeStruct((pieces, rows, 2 * count), BF),
        grid=(1,),
        in_specs=in_specs,
        out_specs=pl.BlockSpec((pieces, rows, count), lambda i: (0, 0, place)),
        input_output_aliases=aliases,
        compiler_params=PARAMS,
        cost_estimate=cost(2 * count * wide * columns, 2 * count * (wide + columns)),
    )(*args)


def sum_lanes_kernel(parts_ref, out_ref):
    for g in range(out_ref.shape[0]):
        lanes = slice(g * 128, (g + 1) * 128)
        total = parts_ref[0, :, lanes].astype(F32)
        for q in range(1, parts_ref.shape[0]):
            total = total + parts_ref[q, :, lanes].astype(F32)
        out_ref[g] = total.astype(BF)


def sum_lanes(parts, steps=2):
    count, rows, lanes = parts.shape
    blocks = lanes // 128
    return pl.pallas_call(
        sum_lanes_kernel,
        out_shape=jax.ShapeDtypeStruct((blocks, rows, 128), BF),
        grid=(steps,),
        in_specs=[pl.BlockSpec((count, rows, lanes // steps), lambda i: (0, 0, i))],
        out_specs=pl.BlockSpec((blocks // steps, rows, 128), lambda i: (i, 0, 0)),
        compiler_params=PARAMS,
        cost_estimate=cost(parts.size, 2 * parts.size),
    )(parts)


def sum_kernel(parts_ref, out_ref):
    total = parts_ref[0].astype(F32)
    for q in range(1, parts_ref.shape[0]):
        total = total + parts_ref[q].astype(F32)
    total = total.astype(BF)
    for q in range(out_ref.shape[0]):
        out_ref[q] = total


def sum_parts(parts, copies, steps=2):
    count, rows, lanes = parts.shape
    return pl.pallas_call(
        sum_kernel,
        out_shape=jax.ShapeDtypeStruct((copies, rows, lanes), BF),
        grid=(steps,),
        in_specs=[pl.BlockSpec((count, rows // steps, lanes), lambda i: (0, i, 0))],
        out_specs=pl.BlockSpec((copies, rows // steps, lanes), lambda i: (0, i, 0)),
        compiler_params=PARAMS,
        cost_estimate=cost(parts.size, 2 * parts.size),
    )(parts)


def panel_kernel(slab_ref, basis_ref, out_ref):
    count, slots, columns = out_ref.shape
    deep, lanes = basis_ref.shape[1:]
    pieces = columns // lanes
    cores = basis_ref.shape[0] // pieces
    for q in range(pieces):
        total = jnp.zeros((count * slots, lanes), F32)
        for c in range(cores):
            left = slab_ref[:, c * deep : (c + 1) * deep]
            right = basis_ref[q * cores + c]
            total = total + jnp.dot(left, right, preferred_element_type=F32)
        out_ref[:, :, q * lanes : (q + 1) * lanes] = total.reshape(count, slots, lanes)


def panel_part(slab, basis, cores):
    count, slots, deep = slab.shape
    columns = basis.shape[0] // cores * basis.shape[2]
    return pl.pallas_call(
        panel_kernel,
        out_shape=jax.ShapeDtypeStruct((count, slots, columns), F32),
        in_specs=[pl.BlockSpec(memory_space=VMEM)] * 2,
        out_specs=pl.BlockSpec(memory_space=VMEM),
        compiler_params=PARAMS,
        cost_estimate=cost(2 * count * slots * columns * deep, 2 * basis.size),
    )(slab.reshape(count * slots, deep), basis)


def example_kernel(nx, scale, at_ref, left_ref, own_ref, other_ref, out_ref):
    blocks, rows, lanes = left_ref.shape
    slots, columns = own_ref.shape[2:]
    groups = blocks // 2
    per_group = lanes // slots
    slot = lax.broadcasted_iota(jnp.int32, (rows, 2 * lanes), 1)
    owner = (slot % lanes) // slots
    total = jnp.zeros((rows, columns), F32)
    for k in range(groups):
        left = jnp.concatenate([left_ref[k], left_ref[groups + k]], axis=1)
        places = [divmod(k * per_group + j, nx) for j in range(per_group)]
        places = [(xp ^ at_ref[0], reverse(zp ^ at_ref[1], 3)) for zp, xp in places]
        right = jnp.concatenate(
            [own_ref[a, b] for a, b in places] + [other_ref[a, b] for a, b in places], axis=0
        )
        for j in range(per_group):
            picked = jnp.where(owner == j, left, jnp.zeros_like(left))
            one = jnp.dot(picked, right, preferred_element_type=F32)
            total = total + one * one
    total = total * scale
    wide = out_ref.shape[2]
    for q in range(out_ref.shape[0]):
        out_ref[q] = total[:, q * wide : (q + 1) * wide]


def examples(at, left, own, other, nx, scale):
    blocks, rows, lanes = left.shape
    columns = own.shape[-1]
    return pl.pallas_call(
        functools.partial(example_kernel, nx, scale),
        out_shape=jax.ShapeDtypeStruct((nx, rows, columns // nx), F32),
        in_specs=[pl.BlockSpec(memory_space=SMEM)] + [pl.BlockSpec(memory_space=VMEM)] * 3,
        out_specs=pl.BlockSpec(memory_space=VMEM),
        compiler_params=PARAMS,
        cost_estimate=cost(2 * blocks * lanes * rows * columns, 4 * own.size),
    )(at, left, own, other)


def per_device(grads_out, inputs, basis_out, basis_in, lengths):
    nz, nx, ny, nc = (lax.axis_size(a) for a in ("z", "x", "y", "c"))
    iz, ix, iy, ic = (lax.axis_index(a) for a in ("z", "x", "y", "c"))
    slots = grads_out.shape[0]
    half = slots // nc
    wide, columns = basis_out.shape
    deep = basis_in.shape[0]
    at = jnp.stack([ix, iz]).astype(jnp.int32)
    tie = lax.optimization_barrier

    blocks = split_rows(grads_out, lengths, half, nz * nx)
    with jax.named_scope("rows_dp"):
        own = exchange(blocks, DP).reshape(nz * nx * half, wide)

    with jax.named_scope("basis_xc"):
        basis_x = lax.all_gather(basis_in, ("x", "c"), axis=0)
    slab = lax.dynamic_slice(inputs, (ic * half, iy * nc * deep), (half, nc * deep))[None]
    with jax.named_scope("slab_z"):
        more_slab = swap(slab, "z", 4)
        own, more_slab = tie((own, more_slab))
        slab = jnp.concatenate([slab, more_slab], axis=0)
        more_slab = swap(slab, "z", 2)

    with jax.named_scope("rows_c"):
        other = swap(own, "c", 1)
    parts = rotate(own, basis_out, 0, nx)
    other, more_slab = tie((other, more_slab))
    parts = rotate(other, basis_out, 1, nx, parts)
    with jax.named_scope("sum_x"):
        parts = exchange(parts, "x")

    with jax.named_scope("slab_z"):
        slab = jnp.concatenate([slab, more_slab], axis=0)
        slab = jnp.concatenate([slab, swap(slab, "z", 1)], axis=0)
    piece = panel_part(slab, basis_x, nc)
    with jax.named_scope("panel_sum"):
        piece = add_from(piece, "y", 1)
        piece = add_from(piece, "y", 2)
    parts, piece = tie((parts, piece))
    parts = sum_lanes(parts)
    with jax.named_scope("sum_z"):
        parts = exchange(parts, "z")
    with jax.named_scope("panel_sum"):
        piece = add_from(piece, "y", 4).astype(BF)
    rotated = sum_parts(parts, nz)
    with jax.named_scope("rotated_z"):
        rotated = exchange(rotated, "z")
    with jax.named_scope("panel_x"):
        piece = jnp.stack([piece] + [swap(piece, "x", k) for k in range(1, 4)])
    with jax.named_scope("panel_c"):
        piece_other = swap(piece, "c", 1)

    result = examples(at, rotated, piece, piece_other, nx, 1.0 / (nz * nx * slots))
    with jax.named_scope("out_x"):
        result = exchange(result, "x")
    return result.reshape(columns, result.shape[2])


def solution(mesh):
    fine = Mesh(mesh.devices.reshape(8, 4, 8, 2), ("z", "x", "y", "c"))
    placed = (P(DP, None), P(DP, None), P(DP, TN), P(TN, DP), P(DP))
    return jax.shard_map(
        per_device, mesh=fine, in_specs=placed, out_specs=P(TN, DP), check_vma=False
    )
```

```python
import functools

import jax
import jax.numpy as jnp
from jax import lax
from jax.experimental import pallas as pl
from jax.experimental.pallas import tpu as pltpu
from jax.sharding import Mesh, PartitionSpec as P

BF = jnp.bfloat16
F32 = jnp.float32
DP = ("z", "x")
TN = ("y", "c")
MIB = 1024 * 1024
PARAMS = pltpu.CompilerParams(vmem_limit_bytes=40 * MIB)
SMEM = pltpu.SMEM
VMEM = pltpu.VMEM


def exchange(blocks, axis):
    return lax.all_to_all(blocks, axis, split_axis=0, concat_axis=0, tiled=True)


def swap(block, axis, bit):
    count = lax.axis_size(axis)
    return lax.ppermute(block, axis, [(i, i ^ bit) for i in range(count)])


def reverse(index, width):
    result = 0
    for k in range(width):
        result = result | (((index >> k) & 1) << (width - 1 - k))
    return result


def add_from(block, axis, bit):
    return block + swap(block.astype(BF), axis, bit).astype(F32)


def cost(flops, moved):
    return pl.CostEstimate(flops=flops, bytes_accessed=moved, transcendentals=0)


def split_kernel(length_ref, grads_ref, out_ref, held, sems):
    parts, half, wide = out_ref.shape
    steps, _, chunk = held.shape
    each = parts // steps
    first = lax.axis_index("c") * half
    copies = [
        pltpu.make_async_copy(
            grads_ref.at[pl.ds(first, half), pl.ds(k * chunk, chunk)], held.at[k], sems.at[k]
        )
        for k in range(steps)
    ]
    for copy in copies:
        copy.start()
    slot = first + lax.broadcasted_iota(jnp.int32, (half, wide), 0)
    live = slot < length_ref[0]
    for k in range(steps):
        copies[k].wait()
        for q in range(each):
            piece = held[k, :, q * wide : (q + 1) * wide]
            out_ref[k * each + q] = jnp.where(live, piece, jnp.zeros_like(piece))


def split_rows(grads, length, half, parts, steps=4):
    wide = grads.shape[1] // parts
    return pl.pallas_call(
        split_kernel,
        out_shape=jax.ShapeDtypeStruct((parts, half, wide), grads.dtype),
        in_specs=[pl.BlockSpec(memory_space=SMEM), pl.BlockSpec(memory_space=pl.ANY)],
        out_specs=pl.BlockSpec(memory_space=VMEM),
        scratch_shapes=[
            VMEM((steps, half, grads.shape[1] // steps), grads.dtype),
            pltpu.SemaphoreType.DMA((steps,)),
        ],
        compiler_params=pltpu.CompilerParams(vmem_limit_bytes=58 * MIB),
        cost_estimate=cost(0, 4 * half * grads.shape[1]),
    )(length, grads)


def rotate_kernel(tokens_ref, basis_ref, *rest):
    out_ref = rest[-1]
    product = jnp.dot(tokens_ref[...], basis_ref[...], preferred_element_type=F32)
    pieces, rows, count = out_ref.shape
    for g in range(0, count, 128):
        turned = product[g : g + 128].T.astype(BF)
        for q in range(pieces):
            out_ref[q, :, g : g + 128] = turned[q * rows : (q + 1) * rows]


def rotate(tokens, basis, place, pieces, before=None):
    count, wide = tokens.shape
    columns = basis.shape[1]
    rows = columns // pieces
    in_specs = [
        pl.BlockSpec((count, wide), lambda i: (0, 0)),
        pl.BlockSpec((wide, columns), lambda i: (0, 0)),
    ]
    args = [tokens, basis]
    aliases = {}
    if before is not None:
        in_specs.append(pl.BlockSpec(memory_space=pl.ANY))
        args.append(before)
        aliases = {2: 0}
    return pl.pallas_call(
        rotate_kernel,
        out_shape=jax.ShapeDtypeStruct((pieces, rows, 2 * count), BF),
        grid=(1,),
        in_specs=in_specs,
        out_specs=pl.BlockSpec((pieces, rows, count), lambda i: (0, 0, place)),
        input_output_aliases=aliases,
        compiler_params=PARAMS,
        cost_estimate=cost(2 * count * wide * columns, 2 * count * (wide + columns)),
    )(*args)


def sum_lanes_kernel(parts_ref, out_ref):
    for g in range(out_ref.shape[0]):
        lanes = slice(g * 128, (g + 1) * 128)
        total = parts_ref[0, :, lanes].astype(F32)
        for q in range(1, parts_ref.shape[0]):
            total = total + parts_ref[q, :, lanes].astype(F32)
        out_ref[g] = total.astype(BF)


def sum_lanes(parts, steps=2):
    count, rows, lanes = parts.shape
    blocks = lanes // 128
    return pl.pallas_call(
        sum_lanes_kernel,
        out_shape=jax.ShapeDtypeStruct((blocks, rows, 128), BF),
        grid=(steps,),
        in_specs=[pl.BlockSpec((count, rows, lanes // steps), lambda i: (0, 0, i))],
        out_specs=pl.BlockSpec((blocks // steps, rows, 128), lambda i: (i, 0, 0)),
        compiler_params=PARAMS,
        cost_estimate=cost(parts.size, 2 * parts.size),
    )(parts)


def sum_kernel(parts_ref, out_ref):
    total = parts_ref[0].astype(F32)
    for q in range(1, parts_ref.shape[0]):
        total = total + parts_ref[q].astype(F32)
    total = total.astype(BF)
    for q in range(out_ref.shape[0]):
        out_ref[q] = total


def sum_parts(parts, copies, steps=2):
    count, rows, lanes = parts.shape
    return pl.pallas_call(
        sum_kernel,
        out_shape=jax.ShapeDtypeStruct((copies, rows, lanes), BF),
        grid=(steps,),
        in_specs=[pl.BlockSpec((count, rows // steps, lanes), lambda i: (0, i, 0))],
        out_specs=pl.BlockSpec((copies, rows // steps, lanes), lambda i: (0, i, 0)),
        compiler_params=PARAMS,
        cost_estimate=cost(parts.size, 2 * parts.size),
    )(parts)


def panel_kernel(at_ref, slab_ref, own_ref, other_ref, out_ref):
    count, slots, _ = out_ref.shape
    pieces, deep, lanes = own_ref.shape
    for q in range(pieces):
        place = q ^ at_ref[0]
        total = jnp.dot(slab_ref[:, :deep], own_ref[place], preferred_element_type=F32)
        total = total + jnp.dot(slab_ref[:, deep:], other_ref[place], preferred_element_type=F32)
        out_ref[:, :, q * lanes : (q + 1) * lanes] = total.reshape(count, slots, lanes)


def panel_part(at, slab, own, other):
    count, slots, deep = slab.shape
    columns = own.shape[0] * own.shape[2]
    return pl.pallas_call(
        panel_kernel,
        out_shape=jax.ShapeDtypeStruct((count, slots, columns), F32),
        in_specs=[pl.BlockSpec(memory_space=SMEM)] + [pl.BlockSpec(memory_space=VMEM)] * 3,
        out_specs=pl.BlockSpec(memory_space=VMEM),
        compiler_params=PARAMS,
        cost_estimate=cost(2 * count * slots * columns * deep, 4 * own.size),
    )(at, slab.reshape(count * slots, deep), own, other)


def example_kernel(nx, scale, at_ref, left_ref, own_ref, other_ref, out_ref):
    blocks, rows, lanes = left_ref.shape
    slots, columns = own_ref.shape[2:]
    groups = blocks // 2
    per_group = lanes // slots
    slot = lax.broadcasted_iota(jnp.int32, (rows, 2 * lanes), 1)
    owner = (slot % lanes) // slots
    total = jnp.zeros((rows, columns), F32)
    for k in range(groups):
        left = jnp.concatenate([left_ref[k], left_ref[groups + k]], axis=1)
        places = [divmod(k * per_group + j, nx) for j in range(per_group)]
        places = [(xp, reverse(zp ^ at_ref[1], 3)) for zp, xp in places]
        right = jnp.concatenate(
            [own_ref[a, b] for a, b in places] + [other_ref[a, b] for a, b in places], axis=0
        )
        for j in range(per_group):
            picked = jnp.where(owner == j, left, jnp.zeros_like(left))
            one = jnp.dot(picked, right, preferred_element_type=F32)
            total = total + one * one
    total = total * scale
    wide = out_ref.shape[2]
    for q in range(out_ref.shape[0]):
        out_ref[q] = total[:, q * wide : (q + 1) * wide]


def examples(at, left, own, other, nx, scale):
    blocks, rows, lanes = left.shape
    columns = own.shape[-1]
    return pl.pallas_call(
        functools.partial(example_kernel, nx, scale),
        out_shape=jax.ShapeDtypeStruct((nx, rows, columns // nx), F32),
        in_specs=[pl.BlockSpec(memory_space=SMEM)] + [pl.BlockSpec(memory_space=VMEM)] * 3,
        out_specs=pl.BlockSpec(memory_space=VMEM),
        compiler_params=PARAMS,
        cost_estimate=cost(2 * blocks * lanes * rows * columns, 4 * own.size),
    )(at, left, own, other)


def per_device(grads_out, inputs, basis_out, basis_in, lengths):
    nz, nx, ny, nc = (lax.axis_size(a) for a in ("z", "x", "y", "c"))
    iz, ix, iy, ic = (lax.axis_index(a) for a in ("z", "x", "y", "c"))
    slots = grads_out.shape[0]
    half = slots // nc
    wide, columns = basis_out.shape
    deep = basis_in.shape[0]
    at = jnp.stack([ix, iz]).astype(jnp.int32)
    tie = lax.optimization_barrier

    blocks = split_rows(grads_out, lengths, half, nz * nx)
    with jax.named_scope("rows_dp"):
        own = exchange(blocks, DP).reshape(nz * nx * half, wide)

    def features(cr):
        start = (iy * nc + (ic ^ cr)) * deep
        return lax.dynamic_slice(inputs, (ic * half, start), (half, deep))

    slab = jnp.concatenate([features(0), features(1)], axis=1)[None]
    with jax.named_scope("slab_z"):
        more_slab = swap(slab, "z", 4)
    with jax.named_scope("basis_x"):
        basis_x = jnp.stack([basis_in] + [swap(basis_in, "x", k) for k in range(1, nx)])
    own, more_slab, basis_x = tie((own, more_slab, basis_x))
    with jax.named_scope("rows_c"):
        other = swap(own, "c", 1)
    parts = rotate(own, basis_out, 0, nx)
    slab = jnp.concatenate([slab, more_slab], axis=0)
    parts, slab, basis_x = tie((parts, slab, basis_x))
    with jax.named_scope("slab_z"):
        more_slab = swap(slab, "z", 2)
    with jax.named_scope("basis_c"):
        more_basis = swap(basis_x, "c", 1)
    parts = rotate(other, basis_out, 1, nx, parts)
    parts, more_slab, more_basis = tie((parts, more_slab, more_basis))
    with jax.named_scope("sum_x"):
        parts = exchange(parts, "x")

    with jax.named_scope("slab_z"):
        slab = jnp.concatenate([slab, more_slab], axis=0)
        slab = jnp.concatenate([slab, swap(slab, "z", 1)], axis=0)
    piece = panel_part(at, slab, basis_x, more_basis)
    with jax.named_scope("panel_sum"):
        piece = add_from(piece, "y", 1)
        piece = add_from(piece, "y", 2)
    parts, piece = tie((parts, piece))
    parts = sum_lanes(parts)
    with jax.named_scope("sum_z"):
        parts = exchange(parts, "z")
    with jax.named_scope("panel_sum"):
        piece = add_from(piece, "y", 4).astype(BF)
    rotated = sum_parts(parts, nz)
    with jax.named_scope("rotated_z"):
        rotated = exchange(rotated, "z")
    with jax.named_scope("panel_x"):
        piece = lax.all_gather(piece, "x", axis=0)
    with jax.named_scope("panel_c"):
        piece_other = swap(piece, "c", 1)

    result = examples(at, rotated, piece, piece_other, nx, 1.0 / (nz * nx * slots))
    with jax.named_scope("out_x"):
        result = exchange(result, "x")
    return result.reshape(columns, result.shape[2])


def solution(mesh):
    fine = Mesh(mesh.devices.reshape(8, 4, 8, 2), ("z", "x", "y", "c"))
    placed = (P(DP, None), P(DP, None), P(DP, TN), P(TN, DP), P(DP))
    return jax.shard_map(
        per_device, mesh=fine, in_specs=placed, out_specs=P(TN, DP), check_vma=False
    )
```

```python
import functools

import jax
import jax.numpy as jnp
from jax import lax
from jax.experimental import pallas as pl
from jax.experimental.pallas import tpu as pltpu
from jax.sharding import Mesh, PartitionSpec as P

BF = jnp.bfloat16
F32 = jnp.float32
DP = ("z", "x")
TN = ("y", "c")
MIB = 1024 * 1024
PARAMS = pltpu.CompilerParams(vmem_limit_bytes=32 * MIB)
SMEM = pltpu.SMEM
VMEM = pltpu.VMEM


def exchange(blocks, axis):
    return lax.all_to_all(blocks, axis, split_axis=0, concat_axis=0, tiled=True)


def swap(block, axis, bit):
    count = lax.axis_size(axis)
    return lax.ppermute(block, axis, [(i, i ^ bit) for i in range(count)])


def reverse(index, width):
    result = 0
    for k in range(width):
        result = result | (((index >> k) & 1) << (width - 1 - k))
    return result


def add_from(block, axis, bit):
    return block + swap(block.astype(BF), axis, bit).astype(F32)


def cost(flops, moved):
    return pl.CostEstimate(flops=flops, bytes_accessed=moved, transcendentals=0)


def split_kernel(length_ref, grads_ref, out_ref, held, sems):
    parts, half, wide = out_ref.shape
    steps, _, chunk = held.shape
    each = parts // steps
    first = lax.axis_index("c") * half
    copies = [
        pltpu.make_async_copy(
            grads_ref.at[pl.ds(first, half), pl.ds(k * chunk, chunk)], held.at[k], sems.at[k]
        )
        for k in range(steps)
    ]
    for copy in copies:
        copy.start()
    slot = first + lax.broadcasted_iota(jnp.int32, (half, wide), 0)
    live = slot < length_ref[0]
    for k in range(steps):
        copies[k].wait()
        for q in range(each):
            piece = held[k, :, q * wide : (q + 1) * wide]
            out_ref[k * each + q] = jnp.where(live, piece, jnp.zeros_like(piece))


def split_rows(grads, length, half, parts, steps=4):
    wide = grads.shape[1] // parts
    return pl.pallas_call(
        split_kernel,
        out_shape=jax.ShapeDtypeStruct((parts, half, wide), grads.dtype),
        in_specs=[pl.BlockSpec(memory_space=SMEM), pl.BlockSpec(memory_space=pl.ANY)],
        out_specs=pl.BlockSpec(memory_space=VMEM),
        scratch_shapes=[
            VMEM((steps, half, grads.shape[1] // steps), grads.dtype),
            pltpu.SemaphoreType.DMA((steps,)),
        ],
        compiler_params=pltpu.CompilerParams(vmem_limit_bytes=58 * MIB),
        cost_estimate=cost(0, 4 * half * grads.shape[1]),
    )(length, grads)


def rotate_kernel(tokens_ref, basis_ref, *rest):
    out_ref = rest[-1]
    count, slots, wide = tokens_ref.shape
    tokens = tokens_ref[...].reshape(count * slots, wide)
    product = jnp.dot(tokens, basis_ref[...], preferred_element_type=F32)
    pieces = out_ref.shape[0]
    for q in range(pieces):
        rows = [product[k * slots : (k + 1) * slots] for k in range(q, count, pieces)]
        out_ref[q] = jnp.concatenate(rows, axis=0).T.astype(BF)


def rotate(tokens, basis, place, pieces, before=None):
    count, slots, wide = tokens.shape
    columns = basis.shape[1]
    lanes = count * slots // pieces
    in_specs = [
        pl.BlockSpec((count, slots, wide), lambda i: (0, 0, 0)),
        pl.BlockSpec((wide, columns), lambda i: (0, 0)),
    ]
    args = [tokens, basis]
    aliases = {}
    if before is not None:
        in_specs.append(pl.BlockSpec(memory_space=pl.ANY))
        args.append(before)
        aliases = {2: 0}
    return pl.pallas_call(
        rotate_kernel,
        out_shape=jax.ShapeDtypeStruct((pieces, columns, 2 * lanes), BF),
        grid=(1,),
        in_specs=in_specs,
        out_specs=pl.BlockSpec((pieces, columns, lanes), lambda i: (0, 0, place)),
        input_output_aliases=aliases,
        compiler_params=PARAMS,
        cost_estimate=cost(2 * count * slots * wide * columns, 2 * count * slots * (wide + columns)),
    )(*args)


def sum_kernel(scale, parts_ref, out_ref):
    total = parts_ref[0].astype(F32)
    for q in range(1, parts_ref.shape[0]):
        total = total + parts_ref[q].astype(F32)
    if scale is not None:
        total = total * scale
    total = total.astype(out_ref.dtype)
    if len(out_ref.shape) == 2:
        out_ref[...] = total
    else:
        for q in range(out_ref.shape[0]):
            out_ref[q] = total


def sum_parts(parts, copies=None, steps=1, dtype=BF, scale=None):
    count, rows, lanes = parts.shape
    block = (rows // steps, lanes)
    if copies is None:
        shape, out_spec = (rows, lanes), pl.BlockSpec(block, lambda i: (i, 0))
    else:
        shape = (copies, rows, lanes)
        out_spec = pl.BlockSpec((copies,) + block, lambda i: (0, i, 0))
    return pl.pallas_call(
        functools.partial(sum_kernel, scale),
        out_shape=jax.ShapeDtypeStruct(shape, dtype),
        grid=(steps,),
        in_specs=[pl.BlockSpec((count,) + block, lambda i: (0, i, 0))],
        out_specs=out_spec,
        compiler_params=PARAMS,
        cost_estimate=cost(parts.size, 2 * parts.size),
    )(parts)


def panel_kernel(at_ref, slab_ref, *refs):
    *basis_refs, out_ref = refs
    count, slots, _ = out_ref.shape
    cores, deep, lanes = basis_refs[0].shape
    for k, basis_ref in enumerate(basis_refs):
        total = jnp.zeros((count * slots, lanes), F32)
        for r in range(cores):
            left = slab_ref[:, r * deep : (r + 1) * deep]
            total = total + jnp.dot(left, basis_ref[r], preferred_element_type=F32)
        start = pl.multiple_of((k ^ at_ref[0]) * lanes, lanes)
        out_ref[:, :, pl.ds(start, lanes)] = total.reshape(count, slots, lanes)


def panel_part(at, slab, bases):
    count, slots, deep = slab.shape
    columns = len(bases) * bases[0].shape[2]
    return pl.pallas_call(
        panel_kernel,
        out_shape=jax.ShapeDtypeStruct((count, slots, columns), F32),
        in_specs=[pl.BlockSpec(memory_space=SMEM)]
        + [pl.BlockSpec(memory_space=VMEM)] * (1 + len(bases)),
        out_specs=pl.BlockSpec(memory_space=VMEM),
        compiler_params=PARAMS,
        cost_estimate=cost(2 * count * slots * columns * deep, 8 * bases[0].size),
    )(at, slab.reshape(count * slots, deep), *bases)


def example_kernel(at_ref, left_ref, own_ref, other_ref, out_ref):
    rows, lanes = left_ref.shape
    count, slots, columns = own_ref.shape
    places = [reverse(k ^ at_ref[1], 3) for k in range(count)]
    right = jnp.concatenate([own_ref[k] for k in places] + [other_ref[k] for k in places], axis=0)
    tile = 128
    slot = lax.broadcasted_iota(jnp.int32, (tile, lanes), 1)
    owner = (slot % (lanes // 2)) // slots
    wide = out_ref.shape[2]
    for n in range(0, columns, 256):
        weights = right[:, n : n + 256]
        for r in range(0, rows, tile):
            left = left_ref[r : r + tile]
            total = jnp.zeros((tile, 256), F32)
            for j in range(count):
                picked = jnp.where(owner == j, left, jnp.zeros_like(left))
                one = jnp.dot(picked, weights, preferred_element_type=F32)
                total = total + one * one
            total = total.astype(out_ref.dtype)
            for q in range(0, 256, wide):
                out_ref[(n + q) // wide, r : r + tile] = total[:, q : q + wide]


def examples(at, left, own, other, nx):
    rows, lanes = left.shape
    columns = own.shape[-1]
    return pl.pallas_call(
        example_kernel,
        out_shape=jax.ShapeDtypeStruct((nx, rows, columns // nx), BF),
        in_specs=[pl.BlockSpec(memory_space=SMEM)] + [pl.BlockSpec(memory_space=VMEM)] * 3,
        out_specs=pl.BlockSpec(memory_space=VMEM),
        compiler_params=PARAMS,
        cost_estimate=cost(2 * lanes * rows * columns, 4 * own.size),
    )(at, left, own, other)


def per_device(grads_out, inputs, basis_out, basis_in, lengths):
    nz, nx, ny, nc = (lax.axis_size(a) for a in ("z", "x", "y", "c"))
    iz, ix, iy, ic = (lax.axis_index(a) for a in ("z", "x", "y", "c"))
    slots = grads_out.shape[0]
    half = slots // nc
    wide, columns = basis_out.shape
    deep = basis_in.shape[0]
    at = jnp.stack([ix, iz]).astype(jnp.int32)
    tie = lax.optimization_barrier

    blocks = split_rows(grads_out, lengths, half, nz * nx)
    with jax.named_scope("rows_dp"):
        own = exchange(blocks, DP)

    def features(cr):
        start = (iy * nc + (ic ^ cr)) * deep
        return lax.dynamic_slice(inputs, (ic * half, start), (half, deep))

    slab = jnp.concatenate([features(0), features(1)], axis=1)[None]
    with jax.named_scope("slab_z"):
        more_slab = swap(slab, "z", 4)
    with jax.named_scope("basis_cx"):
        pair = jnp.stack([basis_in, swap(basis_in, "c", 1)])
        basis_x = [pair] + [swap(pair, "x", k) for k in range(1, nx)]
    own, more_slab, *basis_x = tie((own, more_slab, *basis_x))
    with jax.named_scope("rows_c"):
        other = swap(own, "c", 1)
    parts = rotate(own, basis_out, 0, nx)
    slab = jnp.concatenate([slab, more_slab], axis=0)
    parts = rotate(other, basis_out, 1, nx, parts)
    parts, slab = tie((parts, slab))
    with jax.named_scope("sum_xz"):
        parts = exchange(parts.reshape(nx * nz, columns // nz, parts.shape[2]), ("x", "z"))

    with jax.named_scope("slab_z"):
        slab = jnp.concatenate([slab, swap(slab, "z", 2)], axis=0)
        slab = jnp.concatenate([slab, swap(slab, "z", 1)], axis=0)
    piece = panel_part(at, slab, basis_x)
    with jax.named_scope("panel_sum"):
        piece = add_from(piece, "y", 1)
        piece = add_from(piece, "y", 4)
    parts, piece = tie((parts, piece))
    with jax.named_scope("panel_sum"):
        piece = add_from(piece, "y", 2).astype(BF)
    with jax.named_scope("panel_c"):
        piece_other = swap(piece, "c", 1)
    rotated = sum_parts(parts, copies=nz)
    with jax.named_scope("rotated_z"):
        rotated = exchange(rotated, "z").reshape(columns, parts.shape[2])

    result = examples(at, rotated, piece, piece_other, nx)
    with jax.named_scope("out_x"):
        result = exchange(result, "x")
    return sum_parts(result, dtype=F32, scale=1.0 / (nz * nx * slots))


def solution(mesh):
    fine = Mesh(mesh.devices.reshape(8, 4, 8, 2), ("z", "x", "y", "c"))
    placed = (P(DP, None), P(DP, None), P(DP, TN), P(TN, DP), P(DP))
    return jax.shard_map(
        per_device, mesh=fine, in_specs=placed, out_specs=P(TN, DP), check_vma=False
    )
```

```python
import functools

import jax
import jax.numpy as jnp
from jax import lax
from jax.experimental import pallas as pl
from jax.experimental.pallas import tpu as pltpu
from jax.sharding import Mesh, PartitionSpec as P

BF = jnp.bfloat16
F32 = jnp.float32
DP = ("z", "x")
TN = ("y", "c")
MIB = 1024 * 1024
PARAMS = pltpu.CompilerParams(vmem_limit_bytes=32 * MIB)
SMEM = pltpu.SMEM
VMEM = pltpu.VMEM


def exchange(blocks, axis):
    return lax.all_to_all(blocks, axis, split_axis=0, concat_axis=0, tiled=True)


def swap(block, axis, bit):
    count = lax.axis_size(axis)
    return lax.ppermute(block, axis, [(i, i ^ bit) for i in range(count)])


def reverse(index, width):
    result = 0
    for k in range(width):
        result = result | (((index >> k) & 1) << (width - 1 - k))
    return result


def add_from(block, axis, bit, kind=F32):
    return block + swap(block.astype(kind), axis, bit).astype(F32)


def cost(flops, moved):
    return pl.CostEstimate(flops=flops, bytes_accessed=moved, transcendentals=0)


def split_kernel(length_ref, grads_ref, out_ref, held, ready, sems, out_sems):
    parts, half, wide = out_ref.shape
    steps, _, chunk = held.shape
    each = parts // steps
    first = lax.axis_index("c") * half
    copies = [
        pltpu.make_async_copy(
            grads_ref.at[pl.ds(first, half), pl.ds(k * chunk, chunk)], held.at[k], sems.at[k]
        )
        for k in range(steps)
    ]
    stores = [
        pltpu.make_async_copy(
            ready.at[k], out_ref.at[pl.ds(k * each, each)], out_sems.at[k]
        )
        for k in range(steps)
    ]
    for copy in copies:
        copy.start()
    slot = first + lax.broadcasted_iota(jnp.int32, (half, wide), 0)
    live = slot < length_ref[0]
    for k in range(steps):
        copies[k].wait()
        for q in range(each):
            piece = held[k, :, q * wide : (q + 1) * wide]
            ready[k, q] = jnp.where(live, piece, jnp.zeros_like(piece))
        stores[k].start()
    for store in stores:
        store.wait()


def split_rows(grads, length, half, parts, steps=4):
    wide = grads.shape[1] // parts
    return pl.pallas_call(
        split_kernel,
        out_shape=jax.ShapeDtypeStruct((parts, half, wide), grads.dtype),
        in_specs=[pl.BlockSpec(memory_space=SMEM), pl.BlockSpec(memory_space=pl.ANY)],
        out_specs=pl.BlockSpec(memory_space=pl.ANY),
        scratch_shapes=[
            VMEM((steps, half, grads.shape[1] // steps), grads.dtype),
            VMEM((steps, parts // steps, half, wide), grads.dtype),
            pltpu.SemaphoreType.DMA((steps,)),
            pltpu.SemaphoreType.DMA((steps,)),
        ],
        compiler_params=pltpu.CompilerParams(vmem_limit_bytes=58 * MIB),
        cost_estimate=cost(0, 4 * half * grads.shape[1]),
    )(length, grads)


def rotate_kernel(tokens_ref, basis_ref, *rest):
    out_ref = rest[-1]
    count, slots, wide = tokens_ref.shape
    tokens = tokens_ref[...].reshape(count * slots, wide)
    product = jnp.dot(tokens, basis_ref[...], preferred_element_type=F32)
    pieces = out_ref.shape[0]
    for q in range(pieces):
        rows = [product[k * slots : (k + 1) * slots] for k in range(q, count, pieces)]
        out_ref[q] = jnp.concatenate(rows, axis=0).T.astype(BF)


def rotate(tokens, basis, place, pieces, before=None):
    count, slots, wide = tokens.shape
    columns = basis.shape[1]
    lanes = count * slots // pieces
    in_specs = [
        pl.BlockSpec((count, slots, wide), lambda i: (0, 0, 0)),
        pl.BlockSpec((wide, columns), lambda i: (0, 0)),
    ]
    args = [tokens, basis]
    aliases = {}
    if before is not None:
        in_specs.append(pl.BlockSpec(memory_space=pl.ANY))
        args.append(before)
        aliases = {2: 0}
    return pl.pallas_call(
        rotate_kernel,
        out_shape=jax.ShapeDtypeStruct((pieces, columns, 2 * lanes), BF),
        grid=(1,),
        in_specs=in_specs,
        out_specs=pl.BlockSpec((pieces, columns, lanes), lambda i: (0, 0, place)),
        input_output_aliases=aliases,
        compiler_params=PARAMS,
        cost_estimate=cost(2 * count * slots * wide * columns, 2 * count * slots * (wide + columns)),
    )(*args)


def sum_kernel(scale, parts_ref, out_ref):
    total = parts_ref[0].astype(F32)
    for q in range(1, parts_ref.shape[0]):
        total = total + parts_ref[q].astype(F32)
    if scale is not None:
        total = total * scale
    total = total.astype(out_ref.dtype)
    if len(out_ref.shape) == 2:
        out_ref[...] = total
    else:
        for q in range(out_ref.shape[0]):
            out_ref[q] = total


def sum_parts(parts, copies=None, steps=1, dtype=BF, scale=None):
    count, rows, lanes = parts.shape
    block = (rows // steps, lanes)
    if copies is None:
        shape, out_spec = (rows, lanes), pl.BlockSpec(block, lambda i: (i, 0))
    else:
        shape = (copies, rows, lanes)
        out_spec = pl.BlockSpec((copies,) + block, lambda i: (0, i, 0))
    return pl.pallas_call(
        functools.partial(sum_kernel, scale),
        out_shape=jax.ShapeDtypeStruct(shape, dtype),
        grid=(steps,),
        in_specs=[pl.BlockSpec((count,) + block, lambda i: (0, i, 0))],
        out_specs=out_spec,
        compiler_params=PARAMS,
        cost_estimate=cost(parts.size, 2 * parts.size),
    )(parts)


def panel_kernel(at_ref, slab_ref, other_ref, *refs):
    *own_refs, out_ref = refs
    count, slots, _ = out_ref.shape
    deep, lanes = own_refs[0].shape
    for k, own_ref in enumerate(own_refs):
        total = jnp.dot(slab_ref[:, :deep], own_ref[...], preferred_element_type=F32)
        total = total + jnp.dot(slab_ref[:, deep:], other_ref[k], preferred_element_type=F32)
        start = pl.multiple_of((k ^ at_ref[0]) * lanes, lanes)
        out_ref[:, :, pl.ds(start, lanes)] = total.reshape(count, slots, lanes)


def panel_part(at, slab, other, own):
    count, slots, deep = slab.shape
    columns = len(own) * own[0].shape[1]
    return pl.pallas_call(
        panel_kernel,
        out_shape=jax.ShapeDtypeStruct((count, slots, columns), F32),
        in_specs=[pl.BlockSpec(memory_space=SMEM)]
        + [pl.BlockSpec(memory_space=VMEM)] * (2 + len(own)),
        out_specs=pl.BlockSpec(memory_space=VMEM),
        compiler_params=PARAMS,
        cost_estimate=cost(2 * count * slots * columns * deep, 4 * other.size),
    )(at, slab.reshape(count * slots, deep), other, *own)


def example_kernel(at_ref, left_ref, own_ref, other_ref, out_ref):
    rows, lanes = left_ref.shape
    count, slots, columns = own_ref.shape
    places = [reverse(k ^ at_ref[1], 3) for k in range(count)]
    right = jnp.concatenate([own_ref[k] for k in places] + [other_ref[k] for k in places], axis=0)
    tile = 128
    slot = lax.broadcasted_iota(jnp.int32, (tile, lanes), 1)
    owner = (slot % (lanes // 2)) // slots
    wide = out_ref.shape[2]
    for n in range(0, columns, 256):
        weights = right[:, n : n + 256]
        for r in range(0, rows, tile):
            left = left_ref[r : r + tile]
            total = jnp.zeros((tile, 256), F32)
            for j in range(count):
                picked = jnp.where(owner == j, left, jnp.zeros_like(left))
                one = jnp.dot(picked, weights, preferred_element_type=F32)
                total = total + one * one
            total = total.astype(out_ref.dtype)
            for q in range(0, 256, wide):
                out_ref[(n + q) // wide, r : r + tile] = total[:, q : q + wide]


def examples(at, left, own, other, nx):
    rows, lanes = left.shape
    columns = own.shape[-1]
    return pl.pallas_call(
        example_kernel,
        out_shape=jax.ShapeDtypeStruct((nx, rows, columns // nx), BF),
        in_specs=[pl.BlockSpec(memory_space=SMEM)] + [pl.BlockSpec(memory_space=VMEM)] * 3,
        out_specs=pl.BlockSpec(memory_space=VMEM),
        compiler_params=PARAMS,
        cost_estimate=cost(2 * lanes * rows * columns, 4 * own.size),
    )(at, left, own, other)


def per_device(grads_out, inputs, basis_out, basis_in, lengths):
    nz, nx, ny, nc = (lax.axis_size(a) for a in ("z", "x", "y", "c"))
    iz, ix, iy, ic = (lax.axis_index(a) for a in ("z", "x", "y", "c"))
    slots = grads_out.shape[0]
    half = slots // nc
    wide, columns = basis_out.shape
    deep = basis_in.shape[0]
    at = jnp.stack([ix, iz]).astype(jnp.int32)
    tie = lax.optimization_barrier

    blocks = split_rows(grads_out, lengths, half, nz * nx)
    with jax.named_scope("rows_dp"):
        own = exchange(blocks, DP)

    def features(cr):
        start = (iy * nc + (ic ^ cr)) * deep
        return lax.dynamic_slice(inputs, (ic * half, start), (half, deep))

    slab = jnp.concatenate([features(0), features(1)], axis=1)[None]
    with jax.named_scope("slab_z"):
        more_slab = swap(slab, "z", 4)
    with jax.named_scope("basis_x"):
        basis_x = [basis_in] + [swap(basis_in, "x", k) for k in range(1, nx)]
    own, more_slab, *basis_x = tie((own, more_slab, *basis_x))
    with jax.named_scope("rows_c"):
        other = swap(own, "c", 1)
    parts = rotate(own, basis_out, 0, nx)
    slab = jnp.concatenate([slab, more_slab], axis=0)
    parts = rotate(other, basis_out, 1, nx, parts)
    parts, slab, *basis_x = tie((parts, slab, *basis_x))
    with jax.named_scope("sum_x"):
        parts = exchange(parts, "x")

    with jax.named_scope("slab_z"):
        slab = jnp.concatenate([slab, swap(slab, "z", 2)], axis=0)
        slab = jnp.concatenate([slab, swap(slab, "z", 1)], axis=0)
    with jax.named_scope("basis_c"):
        other_basis = swap(jnp.stack(basis_x), "c", 1)
    piece = panel_part(at, slab, other_basis, basis_x)
    parts, piece = tie((parts, piece))
    parts = sum_parts(parts, steps=2).reshape(nz, columns // nz, parts.shape[2])
    with jax.named_scope("sum_z"):
        parts = exchange(parts, "z")
    with jax.named_scope("panel_sum"):
        piece = add_from(piece, "y", 1, BF)
        piece = add_from(piece, "y", 4)
        piece = add_from(piece, "y", 2).astype(BF)
    with jax.named_scope("panel_c"):
        piece_other = swap(piece, "c", 1)
    rotated = sum_parts(parts, copies=nz)
    with jax.named_scope("rotated_z"):
        rotated = exchange(rotated, "z").reshape(columns, parts.shape[2])

    result = examples(at, rotated, piece, piece_other, nx)
    with jax.named_scope("out_x"):
        result = exchange(result, "x")
    return sum_parts(result, dtype=F32, scale=1.0 / (nz * nx * slots))


def solution(mesh):
    fine = Mesh(mesh.devices.reshape(8, 4, 8, 2), ("z", "x", "y", "c"))
    placed = (P(DP, None), P(DP, None), P(DP, TN), P(TN, DP), P(DP))
    return jax.shard_map(
        per_device, mesh=fine, in_specs=placed, out_specs=P(TN, DP), check_vma=False
    )
```
